32 devices in a mesh: dp: 2 (over x), expert: 16 (over z, y, core).
Axes of the slice: x: 2, y: 2, z: 4, core: 2. Of those that a mesh axis runs over, the one named last changes fastest.
Arguments:
- tokens: bfloat16 [4096, 1024], P(('dp', 'expert')), may hold values from -6 to 6
- grad_out: bfloat16 [4096, 1024], P(('dp', 'expert')), may hold values from -6 to 6
- expert_ids: int32 [4096, 8], P(('dp', 'expert')), may hold values from 0 to 15, all different within a row; in each aligned block of 128 rows (0 to 127, 128 to 255, ...) at most 72 rows name the same one
- gates: float32 [4096, 8], P(('dp', 'expert')), may hold values from 0.1 to 0.5
- w_in: bfloat16 [16, 1024, 768], P('expert', 'dp'), may hold values from -0.1875 to 0.1875
- w_down: bfloat16 [16, 384, 1024], P('expert', 'dp'), may hold values from -0.3125 to 0.3125
Outputs:
- grad_tokens: bfloat16 [4096, 1024], P(('dp', 'expert'))
- grad_in: float32 [16, 1024, 768], P('expert', 'dp')
- grad_down: float32 [16, 384, 1024], P('expert', 'dp')
The draws below stay inside these ranges and needn't reach their ends.
Inputs may be any that keep to these rules, and one draw needn't show every extreme that they name: `expert_ids`: each token names 8 different experts; among the tokens of one device no expert is named more than 72 times, a bound that some block reaches.
All inputs are finite; a program needn't handle non-finite values.
Results may differ from the reference program's by a relative error of at most 0.015.
Values may be sent and summed in bfloat16 or wider, within the bound.
A program may use at most 64 MiB of HBM per device.

```python
import math
import jax
import jax.numpy as jnp
import numpy as np
from jax import lax

D = 1024
H = 384
TOP = 8
TOK_DEV = 128
EXPERTS = 16
CAP = 72
TOKENS = 4096
N_DP = 2
N_EXPERT = 16


def block_levels(stream_key, extent, split, smallest, largest):
    def one(axis_at, parts):
        draws = jax.random.uniform(jax.random.fold_in(jax.random.fold_in(stream_key, 6), axis_at), (parts,), jnp.float32, smallest / len(split), largest / len(split))
        return jnp.repeat(jnp.exp(draws), extent[axis_at] // parts).reshape((-1,) + (1,) * (len(extent) - axis_at - 1))

    level = one(*split[0])
    for cut in split[1:]:
        level = level * one(*cut)
    return level


def routed_block(rng, own, number, rows, amount, top, most, slope):
    ranking = jax.random.permutation(rng, amount)
    packed, ordinary = shares(amount, rows * top, most, slope, True), shares(amount, rows * top, most, slope, False)
    places = jnp.arange(amount)

    def named(sizes, offset_by):
        used = int((sizes > 0).sum())
        fixed = max(1, used // 4)
        passed = fixed + (places - fixed + offset_by * (used - fixed)) % max(1, amount - fixed)
        return jnp.zeros((amount,), jnp.int32).at[ranking[jnp.where(places < fixed, places, passed)]].set(jnp.asarray(sizes, jnp.int32))

    sizes = jnp.where(number % 4 == 0, named(packed, number // 4), named(ordinary, number - number // 4 - 1))
    mixed = jax.random.permutation(jax.random.fold_in(own, 3), amount)
    giver, taker = mixed[0:amount // 2 * 2:2], mixed[1:amount // 2 * 2:2]
    margin = jnp.minimum(sizes[giver] - 1, most - sizes[taker]) // 2
    margin = jnp.where((giver == ranking[0]) | (taker == ranking[0]) | (sizes[taker] == 0), 0, jnp.maximum(margin, 0))
    passed = jax.random.randint(jax.random.fold_in(own, 4), (amount // 2,), 0, 1 << 20) % (margin + 1)
    sizes = sizes.at[giver].add(-passed).at[taker].add(passed)
    labels = jnp.searchsorted(jnp.cumsum(sizes), jnp.arange(rows * top), side="right").astype(jnp.int32)
    listing = labels.reshape(top, rows).T
    listing = listing[jax.random.permutation(jax.random.fold_in(own, 1), rows)]
    offset_by = jax.random.randint(jax.random.fold_in(own, 2), (rows, 1), 0, top)
    return jnp.take_along_axis(listing, (jnp.arange(top)[None, :] + offset_by) % top, axis=1)


def shares(number_of, total, reach, slope, full):
    weights = [(1 << 20) // math.isqrt(rank ** slope) + 1 for rank in range(1, number_of + 1)]
    largest = reach if full else min(reach, max(-(-total // number_of), total * weights[0] // sum(weights)))
    least = 1 if total - largest >= number_of - 1 else 0
    holding, surplus = [largest] + [least] * (number_of - 1), total - largest - least * (number_of - 1)
    while surplus > 0:
        movable = [i for i in range(1, number_of) if holding[i] < largest] or [i for i in range(1, number_of) if holding[i] < reach]
        mass, budget = sum([weights[i] for i in movable]), surplus
        for i in movable:
            addition = min(reach - holding[i], max(1, budget * weights[i] // mass), surplus)
            holding[i] = holding[i] + addition
            surplus = surplus - addition
    return np.array(holding)


def noise(own_key, shape, deviation, bound, pieces=(), held_as=jnp.bfloat16):
    loudness = block_levels(own_key, shape, pieces, -0.22, 0.18) if pieces else 1.0
    values = jax.random.normal(own_key, shape, jnp.float32) * deviation * loudness
    return jnp.minimum(jnp.maximum(values, -bound), bound).astype(held_as)


def setup_inputs(seed: int = 0) -> dict:
    key_list = jax.random.split(jax.random.key(seed), 7)
    tokens = noise(key_list[0], (TOKENS, D), 1.0, 6.0, ((0, 32),))
    grad_out = noise(key_list[1], (TOKENS, D), 0.5, 6.0, ((0, 32),))
    expert_ids_keys = jax.random.split(jax.random.fold_in(key_list[2], 1), TOKENS // TOK_DEV)
    expert_ids_turns = jax.random.permutation(jax.random.fold_in(key_list[2], 3), TOKENS // TOK_DEV)
    expert_ids = jax.vmap(lambda own, number: routed_block(jax.random.fold_in(key_list[2], 2), own, number, TOK_DEV, EXPERTS, TOP, CAP, 2))(expert_ids_keys, expert_ids_turns).reshape((TOKENS, TOP))
    gates = jnp.clip(jnp.exp(math.log(0.5) - 1.609438 * jax.random.uniform(key_list[3], (TOKENS, TOP), jnp.float32) ** block_levels(key_list[3], (TOKENS, TOP), ((0, 32),), -0.2, 0.2)), 0.1, 0.5)
    w_in = noise(key_list[4], (EXPERTS, D, 2 * H), D ** -0.5, 0.1875, ((0, 16), (1, 2)))
    w_down = noise(key_list[5], (EXPERTS, H, D), H ** -0.5, 0.3125, ((0, 16), (1, 2)))
    return dict(tokens=tokens, grad_out=grad_out, expert_ids=expert_ids, gates=gates, w_in=w_in, w_down=w_down)


def hidden_from(preact):
    half_width = preact.shape[1] // 2
    gate_pre = preact[:, :half_width]
    up_pre = preact[:, half_width:]
    sigmoid_gate = jax.nn.sigmoid(gate_pre)
    return (gate_pre * sigmoid_gate * up_pre).astype(jnp.bfloat16)


def pre_grads(preact, grad_hidden):
    half_width = preact.shape[1] // 2
    gate_pre = preact[:, :half_width]
    up_pre = preact[:, half_width:]
    sigmoid_gate = jax.nn.sigmoid(gate_pre)
    grad_gate = grad_hidden * up_pre * sigmoid_gate * (1.0 + gate_pre * (1.0 - sigmoid_gate))
    grad_up = grad_hidden * gate_pre * sigmoid_gate
    return jnp.concatenate([grad_gate, grad_up], axis=1).astype(jnp.bfloat16)


def contract_first(left, right):
    return lax.dot_general(left, right, (((0,), (0,)), ((), ())), preferred_element_type=jnp.float32)


def contract_last(left, right):
    return lax.dot_general(left, right, (((1,), (1,)), ((), ())), preferred_element_type=jnp.float32)


def reference(tokens, grad_out, expert_ids, gates, w_in, w_down):
    block_total = N_DP * N_EXPERT
    route_rows = TOK_DEV * TOP
    route_total = block_total * route_rows
    block_ids = expert_ids.reshape(block_total, route_rows)
    route_marks = (block_ids[:, :, None] == jnp.arange(EXPERTS, dtype=jnp.int32)[None, None, :]).astype(jnp.int32)
    slot_ranks = jnp.sum((jnp.cumsum(route_marks, axis=1) - 1) * route_marks, axis=2)
    block_index = jnp.arange(block_total, dtype=jnp.int32)[:, None]
    targets = ((block_index * EXPERTS + block_ids) * CAP + slot_ranks).reshape(-1).astype(jnp.int32)
    route_index = jnp.arange(route_total, dtype=jnp.int32)
    slot_table = jnp.full((block_total * EXPERTS * CAP,), route_total, jnp.int32).at[targets].set(route_index)
    slot_table = slot_table.reshape(block_total, EXPERTS, CAP).transpose(1, 0, 2).reshape(EXPERTS, block_total * CAP)
    flat_gates = gates.reshape(-1)
    group_rows = N_EXPERT * CAP

    def expert_step(accumulated, inputs):
        slot_routes, weight_first, weight_second = inputs
        occupied = slot_routes < route_total
        clipped = jnp.minimum(slot_routes, route_total - 1)
        source_rows = (clipped // TOP).astype(jnp.int32)
        slot_tokens = jnp.where(occupied[:, None], tokens[source_rows], jnp.zeros((), jnp.bfloat16))
        slot_gates = jnp.where(occupied, flat_gates[clipped], jnp.zeros((), jnp.float32))
        slot_grads = (slot_gates[:, None] * grad_out[source_rows].astype(jnp.float32)).astype(jnp.bfloat16)
        preact = jnp.dot(slot_tokens, weight_first, preferred_element_type=jnp.float32)
        hidden_act = hidden_from(preact)
        grad_hidden = contract_last(slot_grads, weight_second)
        pre_grad = pre_grads(preact, grad_hidden)
        slot_back = contract_last(pre_grad, weight_first).astype(jnp.bfloat16)
        accumulated = accumulated.at[source_rows].add(
            jnp.where(occupied[:, None], slot_back.astype(jnp.float32), jnp.zeros((), jnp.float32)))
        grad_first = jnp.zeros(weight_first.shape, jnp.float32)
        grad_second = jnp.zeros(weight_second.shape, jnp.float32)
        for group_index in range(N_DP):
            lower = group_index * group_rows
            upper = lower + group_rows
            part_first = contract_first(slot_tokens[lower:upper], pre_grad[lower:upper]).astype(jnp.bfloat16)
            part_second = contract_first(hidden_act[lower:upper], slot_grads[lower:upper]).astype(jnp.bfloat16)
            grad_first = grad_first + lax.optimization_barrier(part_first).astype(jnp.float32)
            grad_second = grad_second + lax.optimization_barrier(part_second).astype(jnp.float32)
        return accumulated, (grad_first, grad_second)

    start_value = jnp.zeros((TOKENS, D), jnp.float32)
    accumulated, (grad_in, grad_down) = lax.scan(expert_step, start_value, (slot_table, w_in, w_down))
    return accumulated.astype(jnp.bfloat16), grad_in, grad_down
```

```python
import functools

import jax
import jax.numpy as jnp
from jax import lax
from jax.experimental import pallas as pl
from jax.experimental.pallas import tpu as pltpu
from jax.sharding import PartitionSpec as P

MESH = pl.DeviceIdType.MESH
F32 = jnp.float32
BF16 = jnp.bfloat16
VMEM_BYTES = 56 * 1024 * 1024


def hidden_from(preact):
    half_width = preact.shape[1] // 2
    gate_pre = preact[:, :half_width]
    up_pre = preact[:, half_width:]
    sigmoid_gate = jax.nn.sigmoid(gate_pre)
    return (gate_pre * sigmoid_gate * up_pre).astype(jnp.bfloat16)


def pre_grads(preact, grad_hidden):
    half_width = preact.shape[1] // 2
    gate_pre = preact[:, :half_width]
    up_pre = preact[:, half_width:]
    sigmoid_gate = jax.nn.sigmoid(gate_pre)
    grad_gate = grad_hidden * up_pre * sigmoid_gate * (1.0 + gate_pre * (1.0 - sigmoid_gate))
    grad_up = grad_hidden * gate_pre * sigmoid_gate
    return jnp.concatenate([grad_gate, grad_up], axis=1).astype(jnp.bfloat16)


def contract_first(left, right):
    return lax.dot_general(
        left, right, (((0,), (0,)), ((), ())), preferred_element_type=jnp.float32
    )


def contract_last(left, right):
    return lax.dot_general(
        left, right, (((1,), (1,)), ((), ())), preferred_element_type=jnp.float32
    )


def on_device(tokens, grad_out, expert_ids, gates, w_in, w_down):
    token_rows, model_width = tokens.shape
    route_width = expert_ids.shape[1]
    expert_count = lax.axis_size("expert")
    route_total = token_rows * route_width
    capacity = route_total // expert_count + max(1, route_total // (8 * expert_count))
    slot_total = expert_count * capacity
    flat_ids = expert_ids.reshape(route_total)
    route_marks = (flat_ids[:, None] == jnp.arange(expert_count, dtype=jnp.int32)[None, :]).astype(
        jnp.int32
    )
    route_index = jnp.arange(route_total, dtype=jnp.int32)
    lower_table = (route_index[None, :] <= route_index[:, None]).astype(jnp.bfloat16)
    running = jnp.dot(
        lower_table, route_marks.astype(jnp.bfloat16), preferred_element_type=jnp.float32
    )
    slot_ranks = jnp.sum((running.astype(jnp.int32) - 1) * route_marks, axis=1)
    targets = flat_ids * capacity + slot_ranks
    route_of_slot = jnp.full((slot_total,), route_total, jnp.int32).at[targets].set(route_index)
    occupied = route_of_slot < route_total
    clipped = jnp.minimum(route_of_slot, route_total - 1)
    source_rows = clipped // route_width
    slot_gates = jnp.where(
        occupied, gates.reshape(route_total)[clipped], jnp.zeros((), jnp.float32)
    )
    send_tokens = jnp.where(occupied[:, None], tokens[source_rows], jnp.zeros((), jnp.bfloat16))
    send_grads = (slot_gates[:, None] * grad_out[source_rows].astype(jnp.float32)).astype(
        jnp.bfloat16
    )
    recv_tokens, recv_grads = (
        lax.all_to_all(
            send_tokens.reshape(expert_count, capacity, model_width),
            "expert",
            split_axis=0,
            concat_axis=0,
            tiled=True,
        ),
        lax.all_to_all(
            send_grads.reshape(expert_count, capacity, model_width),
            "expert",
            split_axis=0,
            concat_axis=0,
            tiled=True,
        ),
    )
    slot_tokens = recv_tokens.reshape(slot_total, model_width)
    slot_grads = recv_grads.reshape(slot_total, model_width)
    local_in = w_in[0]
    local_down = w_down[0]
    full_in, full_down = (
        lax.all_gather(local_in, "dp", axis=0, tiled=True),
        lax.all_gather(local_down, "dp", axis=0, tiled=True),
    )
    preact = jnp.dot(slot_tokens, full_in, preferred_element_type=jnp.float32)
    grad_hidden = contract_last(slot_grads, full_down)
    pre_grad = pre_grads(preact, grad_hidden)
    slot_back = contract_last(pre_grad, full_in).astype(jnp.bfloat16)
    hidden_act = hidden_from(preact)
    columns = slot_tokens
    grad_in_local = lax.psum_scatter(
        contract_first(columns, pre_grad).astype(jnp.bfloat16),
        "dp",
        scatter_dimension=0,
        tiled=True,
    ).astype(jnp.float32)
    columns = hidden_act
    grad_down_local = lax.psum_scatter(
        contract_first(columns, slot_grads).astype(jnp.bfloat16),
        "dp",
        scatter_dimension=0,
        tiled=True,
    ).astype(jnp.float32)
    slot_return = lax.all_to_all(
        slot_back.reshape(expert_count, capacity, model_width),
        "expert",
        split_axis=0,
        concat_axis=0,
        tiled=True,
    )
    per_route = slot_return.reshape(slot_total, model_width)[targets]
    grad_tokens = jnp.sum(
        per_route.reshape(token_rows, route_width, model_width).astype(jnp.float32), axis=1
    ).astype(jnp.bfloat16)
    return (grad_tokens, grad_in_local[None], grad_down_local[None])


def fused_kernel(
    expert_count, capacity,
    ids_ref, gates_ref, tok_in, grad_in, win_in, wdn_in,
    gtok_out, gin_out, gdn_out,
    data, meta, win, wdn, acc_in, acc_dn, sel, xs, gs, act, dpre, part,
    sib_in, y_out, y_in, z_out, z_in, gin_send, gin_recv, gdn_send, gdn_recv,
    local_sem, own_send, fwd_send, y_send, sib_send, recv_sem,
    w_send, w_recv, sib_part_send, sib_part_recv, y_part_send, y_part_recv,
    z_part_send, z_part_recv, g_send, g_recv,
):
    depth = expert_count // 4
    dp = lax.axis_index("dp")
    me = lax.axis_index("expert")
    z, y, c = me // 4, (me // 2) % 2, me % 2
    token_rows, model_width = tok_in.shape
    half_in, half_dn = win_in.shape[0], wdn_in.shape[0]
    half_width = wdn.shape[0]
    slots = 4 * capacity
    tile = model_width // 4

    def block_of(zz, yy, cc):
        return zz * 4 + yy * 2 + cc

    sib, y_peer = block_of(z, y, 1 - c), block_of(z, 1 - y, c)
    table = [sorted(range(depth), key=lambda b: (abs(b - zz), b)) for zz in range(depth)]

    def near(k):
        total = jnp.int32(0)
        for zz in range(depth):
            for kk in range(depth):
                hit = (z == zz).astype(jnp.int32) * (jnp.int32(k) == kk).astype(jnp.int32)
                total = total + hit * table[zz][kk]
        return total

    def data_copy(block, target, sems):
        return (
            pltpu.make_async_remote_copy(
                src_ref=data.at[block], dst_ref=data.at[block],
                send_sem=sems.at[0], recv_sem=recv_sem.at[block, 0],
                device_id=(dp, target), device_id_type=MESH),
            pltpu.make_async_remote_copy(
                src_ref=meta.at[block], dst_ref=meta.at[block],
                send_sem=sems.at[1], recv_sem=recv_sem.at[block, 1],
                device_id=(dp, target), device_id_type=MESH),
        )

    def ship(block, target, sems):
        for copy in data_copy(block, target, sems):
            copy.start()

    def sent(block, target, sems):
        for copy in data_copy(block, target, sems):
            copy.wait_send()

    def arrived(block):
        for copy in data_copy(block, sib, own_send.at[0]):
            copy.wait_recv()

    own_rows_in = pl.ds(pl.multiple_of(dp * half_in, 16), half_in)
    own_rows_dn = pl.ds(pl.multiple_of(dp * half_dn, 16), half_dn)
    peer_rows_dn = pl.ds(pl.multiple_of((1 - dp) * half_dn, 16), half_dn)
    local = [
        pltpu.make_async_copy(tok_in, data.at[me, 0], local_sem.at[0]),
        pltpu.make_async_copy(grad_in, data.at[me, 1], local_sem.at[1]),
        pltpu.make_async_copy(win_in, win.at[own_rows_in], local_sem.at[2]),
        pltpu.make_async_copy(wdn_in, wdn.at[own_rows_dn], local_sem.at[3]),
    ]
    for copy in local:
        copy.start()

    barrier = pltpu.get_barrier_semaphore()
    partners = [(dp, sib), (dp, y_peer), (1 - dp, me)]
    for step in range(1, depth):
        partners.append((dp, block_of((z + step) % depth, y, c)))
    for partner in partners:
        pl.semaphore_signal(barrier, inc=1, device_id=partner, device_id_type=MESH)

    experts = lax.broadcasted_iota(jnp.int32, (expert_count, token_rows), 0)
    marks = jnp.zeros((expert_count, token_rows), F32)
    scale = jnp.zeros((expert_count, token_rows), F32)
    for k in range(ids_ref.shape[0]):
        hit = ids_ref[k : k + 1, :] == experts
        marks = marks + jnp.where(hit, 1.0, 0.0)
        scale = scale + jnp.where(hit, gates_ref[k : k + 1, :], 0.0)
    before = (
        lax.broadcasted_iota(jnp.int32, (token_rows, token_rows), 0)
        < lax.broadcasted_iota(jnp.int32, (token_rows, token_rows), 1)
    )
    ranks = jnp.dot(
        marks.astype(BF16), jnp.where(before, 1.0, 0.0).astype(BF16), preferred_element_type=F32
    )
    meta[me, 0:expert_count, :] = jnp.where(marks > 0.5, ranks, -1.0)
    meta[me, expert_count : 2 * expert_count, :] = scale

    pl.semaphore_wait(barrier, len(partners))

    weights = [
        pltpu.make_async_remote_copy(
            src_ref=src, dst_ref=dst, send_sem=w_send.at[i], recv_sem=w_recv.at[i],
            device_id=(1 - dp, me), device_id_type=MESH)
        for i, (src, dst) in enumerate(
            ((win_in, win.at[own_rows_in]), (wdn_in, wdn.at[own_rows_dn])))
    ]
    local[0].wait()
    local[1].wait()

    @pl.when(z > 0)
    def _():
        ship(me, block_of(jnp.maximum(z - 1, 0), y, c), own_send.at[0])

    @pl.when(z < depth - 1)
    def _():
        ship(me, block_of(jnp.minimum(z + 1, depth - 1), y, c), own_send.at[1])

    ship(me, y_peer, y_send.at[0])
    for copy in weights:
        copy.start()
    ship(me, sib, sib_send.at[0, 0])

    def onward(zz):
        step_to = jnp.where(zz < z, z + 1, z - 1)
        return (step_to >= 0) & (step_to < depth), jnp.clip(step_to, 0, depth - 1)

    def arrivals(k):
        zz = near(k)
        block = block_of(zz, y, c)
        arrived(block)
        more, step_to = onward(zz)

        @pl.when(more)
        def _():
            ship(block, block_of(step_to, y, c), fwd_send.at[k])

        ship(block, y_peer, y_send.at[k])
        ship(block, sib, sib_send.at[k, 0])

    def sib_part(k):
        return pltpu.make_async_remote_copy(
            src_ref=part.at[k, 1 - c], dst_ref=sib_in.at[k],
            send_sem=sib_part_send.at[k], recv_sem=sib_part_recv.at[k],
            device_id=(dp, sib), device_id_type=MESH)

    def y_part(k):
        return pltpu.make_async_remote_copy(
            src_ref=y_out.at[k], dst_ref=y_in.at[k],
            send_sem=y_part_send.at[k], recv_sem=y_part_recv.at[k],
            device_id=(dp, y_peer), device_id_type=MESH)

    def z_part(k, slot):
        return pltpu.make_async_remote_copy(
            src_ref=z_out.at[k], dst_ref=z_in.at[slot],
            send_sem=z_part_send.at[k], recv_sem=z_part_recv.at[slot],
            device_id=(dp, block_of(near(k), y, c)), device_id_type=MESH)

    def gin_part(i):
        rows = pl.ds(pl.multiple_of(i * tile, tile), tile)
        return pltpu.make_async_remote_copy(
            src_ref=gin_send.at[rows], dst_ref=gin_recv.at[rows],
            send_sem=g_send.at[i], recv_sem=g_recv.at[i],
            device_id=(1 - dp, me), device_id_type=MESH)

    half_tiles = half_in // tile
    gdn_part = pltpu.make_async_remote_copy(
        src_ref=gdn_send, dst_ref=gdn_recv,
        send_sem=g_send.at[half_tiles], recv_sem=g_recv.at[half_tiles],
        device_id=(1 - dp, me), device_id_type=MESH)

    def combine_y(k):
        sib_part(k).wait_recv()
        y_out[k] = (
            part[k, c, 1 - y].astype(F32) + sib_in[k, 1 - y].astype(F32)
        ).astype(BF16)
        y_part(k).start()

    def combine_z(k):
        y_part(k).wait_recv()
        z_out[k] = (
            part[k, c, y].astype(F32) + sib_in[k, y].astype(F32) + y_in[k].astype(F32)
        ).astype(BF16)

        @pl.when(k > 0)
        def _():
            z_part(jnp.maximum(k, 1), z).start()

    acc_in[...] = jnp.zeros_like(acc_in)
    acc_dn[...] = jnp.zeros_like(acc_dn)
    for k in range(1, min(3, depth)):
        arrivals(k)
    local[2].wait()
    local[3].wait()

    def chunk(k, carry):
        @pl.when((k >= 1) & (k + 2 < depth))
        def _():
            arrivals(jnp.minimum(k + 2, depth - 1))

        zz = near(k)
        block = block_of(zz, 1 - y, c)
        arrived(block)
        ship(block, sib, sib_send.at[k, 1])
        arrived(block_of(zz, y, 1 - c))
        arrived(block_of(zz, 1 - y, 1 - c))

        @pl.when(k == 0)
        def _():
            for copy in weights:
                copy.wait_recv()

        first = zz * 4
        slot_rows = lax.broadcasted_iota(jnp.int32, (slots, token_rows), 0)
        slot_gate = jnp.zeros((slots, 1), F32)
        for j in range(4):
            rank = meta[first + j, pl.ds(me, 1), :].astype(jnp.int32)
            place = jnp.where(rank >= 0, rank + j * capacity, -1)
            scale_row = meta[first + j, pl.ds(expert_count + me, 1), :]
            hit = slot_rows == place
            slot_gate = slot_gate + jnp.sum(
                jnp.where(hit, scale_row, 0.0), axis=1, keepdims=True
            )
            sel[:, j * token_rows : (j + 1) * token_rows] = jnp.where(hit, 1.0, 0.0).astype(BF16)
        chosen = sel[...]
        chunk_tokens = data[pl.ds(first, 4), 0].reshape(4 * token_rows, model_width)
        xs[...] = jnp.dot(chosen, chunk_tokens, preferred_element_type=F32).astype(BF16)
        chunk_grads = data[pl.ds(first, 4), 1].reshape(4 * token_rows, model_width)
        gs[...] = (
            slot_gate * jnp.dot(chosen, chunk_grads, preferred_element_type=F32)
        ).astype(BF16)
        preact = jnp.dot(xs[...], win[...], preferred_element_type=F32)
        grad_hidden = contract_last(gs[...], wdn[...])
        act[...] = hidden_from(preact)
        dpre[...] = pre_grads(preact, grad_hidden)

        last = k == depth - 1

        @pl.loop(0, 4)
        def _(i):
            at = ((1 - dp) * half_tiles + i) % 4
            rows = pl.ds(pl.multiple_of(at * tile, tile), tile)
            total = acc_in[rows, :] + contract_first(xs[:, rows], dpre[...])
            acc_in[rows, :] = total

            @pl.when(last & (i < half_tiles))
            def _():
                piece = jnp.minimum(i, half_tiles - 1)
                gin_send[pl.ds(pl.multiple_of(piece * tile, tile), tile), :] = total.astype(BF16)
                gin_part(piece).start()

        acc_dn[...] += contract_first(act[...], gs[...])

        @pl.when(last)
        def _():
            gdn_send[...] = acc_dn[peer_rows_dn, :].astype(BF16)
            gdn_part.start()

        back = contract_last(dpre[...], win[...]).astype(BF16)
        spread = contract_first(sel[...], back).astype(BF16)
        for j in range(4):
            part[k, j % 2, j // 2] = spread[j * token_rows : (j + 1) * token_rows]
        sib_part(k).start()

        @pl.when(k >= 1)
        def _():
            combine_y(jnp.maximum(k - 1, 0))

        @pl.when(k >= 2)
        def _():
            combine_z(jnp.maximum(k - 2, 0))

        return carry

    lax.fori_loop(0, depth, chunk, 0)
    combine_y(depth - 1)
    if depth >= 2:
        combine_z(jnp.int32(depth - 2))
    combine_z(jnp.int32(depth - 1))

    total = z_out[0].astype(F32)
    for step in range(1, depth):
        slot = (z + step) % depth
        z_part(step, slot).wait_recv()
        total = total + z_in[slot].astype(F32)
    gtok_out[...] = total.astype(BF16)

    for i in range(half_tiles):
        gin_part(i).wait_recv()
        rows = pl.ds(i * tile, tile)
        own = pl.ds(pl.multiple_of(dp * half_in + i * tile, tile), tile)
        gin_out[rows, :] = acc_in[own, :].astype(BF16).astype(F32) + gin_recv[rows, :].astype(F32)
    gdn_part.wait_recv()
    gdn_out[...] = acc_dn[own_rows_dn, :].astype(BF16).astype(F32) + gdn_recv[...].astype(F32)

    @pl.when(z > 0)
    def _():
        sent(me, sib, own_send.at[0])

    @pl.when(z < depth - 1)
    def _():
        sent(me, sib, own_send.at[1])

    for k in range(depth):
        sent(me, y_peer, y_send.at[k])
        sent(me, sib, sib_send.at[k, 0])
        sent(me, sib, sib_send.at[k, 1])
        sib_part(k).wait_send()
        y_part(k).wait_send()
        if k > 0:
            more, _ = onward(near(k))

            @pl.when(more)
            def _():
                sent(me, sib, fwd_send.at[k])

            z_part(k, z).wait_send()
    for copy in weights:
        copy.wait_send()
    for i in range(half_tiles):
        gin_part(i).wait_send()
    gdn_part.wait_send()


def fused_on_device(tokens, grad_out, expert_ids, gates, w_in, w_down):
    token_rows, model_width = tokens.shape
    route_total = token_rows * expert_ids.shape[1]
    expert_count = lax.axis_size("expert")
    capacity = route_total // expert_count + max(1, route_total // (8 * expert_count))
    depth = expert_count // 4
    slots = 4 * capacity
    half_in, in_width = w_in.shape[1:]
    half_dn = w_down.shape[1]
    half_tiles = half_in // (model_width // 4)
    dma = lambda *shape: pltpu.SemaphoreType.DMA(shape)
    vmem = lambda shape, dtype=BF16: pltpu.VMEM(shape, dtype)
    grad_tokens, grad_in, grad_down = pl.pallas_call(
        functools.partial(fused_kernel, expert_count, capacity),
        out_shape=(
            jax.ShapeDtypeStruct((token_rows, model_width), BF16),
            jax.ShapeDtypeStruct((half_in, in_width), F32),
            jax.ShapeDtypeStruct((half_dn, model_width), F32),
        ),
        in_specs=[pl.BlockSpec(memory_space=pltpu.VMEM)] * 2
        + [pl.BlockSpec(memory_space=pl.ANY)] * 4,
        out_specs=(pl.BlockSpec(memory_space=pltpu.VMEM),) * 3,
        scratch_shapes=[
            vmem((expert_count, 2, token_rows, model_width)),
            vmem((expert_count, 2 * expert_count, token_rows), F32),
            vmem((2 * half_in, in_width)),
            vmem((2 * half_dn, model_width)),
            vmem((2 * half_in, in_width), F32),
            vmem((2 * half_dn, model_width), F32),
            vmem((slots, 4 * token_rows)),
            vmem((slots, model_width)),
            vmem((slots, model_width)),
            vmem((slots, in_width // 2)),
            vmem((slots, in_width)),
            vmem((depth, 2, 2, token_rows, model_width)),
            vmem((depth, 2, token_rows, model_width)),
            vmem((depth, token_rows, model_width)),
            vmem((depth, token_rows, model_width)),
            vmem((depth, token_rows, model_width)),
            vmem((depth, token_rows, model_width)),
            vmem((half_in, in_width)),
            vmem((half_in, in_width)),
            vmem((half_dn, model_width)),
            vmem((half_dn, model_width)),
            dma(4), dma(2, 2), dma(depth, 2), dma(depth, 2), dma(depth, 2, 2),
            dma(expert_count, 2), dma(2), dma(2), dma(depth), dma(depth), dma(depth), dma(depth),
            dma(depth), dma(depth), dma(half_tiles + 1), dma(half_tiles + 1),
        ],
        compiler_params=pltpu.CompilerParams(
            collective_id=0, has_side_effects=True, vmem_limit_bytes=VMEM_BYTES
        ),
    )(expert_ids.T, gates.T, tokens, grad_out, w_in[0], w_down[0])
    return grad_tokens, grad_in[None], grad_down[None]


def fits_fused(mesh):
    return mesh.shape["dp"] == 2 and mesh.shape["expert"] in (8, 16)


def solution(mesh):
    in_specs = (
        P(("dp", "expert"), None),
        P(("dp", "expert"), None),
        P(("dp", "expert"), None),
        P(("dp", "expert"), None),
        P("expert", "dp", None),
        P("expert", "dp", None),
    )
    out_specs = (P(("dp", "expert"), None), P("expert", "dp", None), P("expert", "dp", None))
    return jax.shard_map(
        fused_on_device if fits_fused(mesh) else on_device,
        mesh=mesh, in_specs=in_specs, out_specs=out_specs, check_vma=False
    )
```

```python
import functools

import jax
import jax.numpy as jnp
from jax import lax
from jax.experimental import pallas as pl
from jax.experimental.pallas import tpu as pltpu
from jax.sharding import PartitionSpec as P

MESH = pl.DeviceIdType.MESH
F32 = jnp.float32
BF16 = jnp.bfloat16
VMEM_BYTES = 56 * 1024 * 1024


def hidden_from(preact):
    half_width = preact.shape[1] // 2
    gate_pre = preact[:, :half_width]
    up_pre = preact[:, half_width:]
    sigmoid_gate = jax.nn.sigmoid(gate_pre)
    return (gate_pre * sigmoid_gate * up_pre).astype(jnp.bfloat16)


def pre_grads(preact, grad_hidden):
    half_width = preact.shape[1] // 2
    gate_pre = preact[:, :half_width]
    up_pre = preact[:, half_width:]
    sigmoid_gate = jax.nn.sigmoid(gate_pre)
    grad_gate = grad_hidden * up_pre * sigmoid_gate * (1.0 + gate_pre * (1.0 - sigmoid_gate))
    grad_up = grad_hidden * gate_pre * sigmoid_gate
    return jnp.concatenate([grad_gate, grad_up], axis=1).astype(jnp.bfloat16)


def contract_first(left, right):
    return lax.dot_general(
        left, right, (((0,), (0,)), ((), ())), preferred_element_type=jnp.float32
    )


def contract_last(left, right):
    return lax.dot_general(
        left, right, (((1,), (1,)), ((), ())), preferred_element_type=jnp.float32
    )


def on_device(tokens, grad_out, expert_ids, gates, w_in, w_down):
    token_rows, model_width = tokens.shape
    route_width = expert_ids.shape[1]
    expert_count = lax.axis_size("expert")
    route_total = token_rows * route_width
    capacity = route_total // expert_count + max(1, route_total // (8 * expert_count))
    slot_total = expert_count * capacity
    flat_ids = expert_ids.reshape(route_total)
    route_marks = (flat_ids[:, None] == jnp.arange(expert_count, dtype=jnp.int32)[None, :]).astype(
        jnp.int32
    )
    route_index = jnp.arange(route_total, dtype=jnp.int32)
    lower_table = (route_index[None, :] <= route_index[:, None]).astype(jnp.bfloat16)
    running = jnp.dot(
        lower_table, route_marks.astype(jnp.bfloat16), preferred_element_type=jnp.float32
    )
    slot_ranks = jnp.sum((running.astype(jnp.int32) - 1) * route_marks, axis=1)
    targets = flat_ids * capacity + slot_ranks
    route_of_slot = jnp.full((slot_total,), route_total, jnp.int32).at[targets].set(route_index)
    occupied = route_of_slot < route_total
    clipped = jnp.minimum(route_of_slot, route_total - 1)
    source_rows = clipped // route_width
    slot_gates = jnp.where(
        occupied, gates.reshape(route_total)[clipped], jnp.zeros((), jnp.float32)
    )
    send_tokens = jnp.where(occupied[:, None], tokens[source_rows], jnp.zeros((), jnp.bfloat16))
    send_grads = (slot_gates[:, None] * grad_out[source_rows].astype(jnp.float32)).astype(
        jnp.bfloat16
    )
    recv_tokens, recv_grads = (
        lax.all_to_all(
            send_tokens.reshape(expert_count, capacity, model_width),
            "expert",
            split_axis=0,
            concat_axis=0,
            tiled=True,
        ),
        lax.all_to_all(
            send_grads.reshape(expert_count, capacity, model_width),
            "expert",
            split_axis=0,
            concat_axis=0,
            tiled=True,
        ),
    )
    slot_tokens = recv_tokens.reshape(slot_total, model_width)
    slot_grads = recv_grads.reshape(slot_total, model_width)
    local_in = w_in[0]
    local_down = w_down[0]
    full_in, full_down = (
        lax.all_gather(local_in, "dp", axis=0, tiled=True),
        lax.all_gather(local_down, "dp", axis=0, tiled=True),
    )
    preact = jnp.dot(slot_tokens, full_in, preferred_element_type=jnp.float32)
    grad_hidden = contract_last(slot_grads, full_down)
    pre_grad = pre_grads(preact, grad_hidden)
    slot_back = contract_last(pre_grad, full_in).astype(jnp.bfloat16)
    hidden_act = hidden_from(preact)
    columns = slot_tokens
    grad_in_local = lax.psum_scatter(
        contract_first(columns, pre_grad).astype(jnp.bfloat16),
        "dp",
        scatter_dimension=0,
        tiled=True,
    ).astype(jnp.float32)
    columns = hidden_act
    grad_down_local = lax.psum_scatter(
        contract_first(columns, slot_grads).astype(jnp.bfloat16),
        "dp",
        scatter_dimension=0,
        tiled=True,
    ).astype(jnp.float32)
    slot_return = lax.all_to_all(
        slot_back.reshape(expert_count, capacity, model_width),
        "expert",
        split_axis=0,
        concat_axis=0,
        tiled=True,
    )
    per_route = slot_return.reshape(slot_total, model_width)[targets]
    grad_tokens = jnp.sum(
        per_route.reshape(token_rows, route_width, model_width).astype(jnp.float32), axis=1
    ).astype(jnp.bfloat16)
    return (grad_tokens, grad_in_local[None], grad_down_local[None])


def fused_kernel(
    expert_count, capacity,
    ids_ref, gates_ref, tok_in, grad_in, win_in, wdn_in,
    z_in, gin_own, gin_recv, gdn_own, gdn_recv,
    data, meta, win, wdn, acc_dn, sel, xs, gs, act, dpre, part,
    sib_in, y_out, y_in, z_out, gin_send, gdn_send,
    local_sem, own_send, fwd_send, y_send, sib_send, recv_sem,
    w_send, w_recv, sib_part_send, sib_part_recv, y_part_send, y_part_recv,
    z_part_send, z_part_recv, g_send, g_recv,
):
    depth = expert_count // 4
    dp = lax.axis_index("dp")
    me = lax.axis_index("expert")
    z, y, c = me // 4, (me // 2) % 2, me % 2
    token_rows, model_width = tok_in.shape
    half_in, half_dn = win_in.shape[0], wdn_in.shape[0]
    half_width = wdn.shape[0]
    slots = 4 * capacity
    tile = model_width // 4

    def block_of(zz, yy, cc):
        return zz * 4 + yy * 2 + cc

    sib, y_peer = block_of(z, y, 1 - c), block_of(z, 1 - y, c)
    table = [sorted(range(depth), key=lambda b: (abs(b - zz), b)) for zz in range(depth)]

    def near(k):
        total = jnp.int32(0)
        for zz in range(depth):
            for kk in range(depth):
                hit = (z == zz).astype(jnp.int32) * (jnp.int32(k) == kk).astype(jnp.int32)
                total = total + hit * table[zz][kk]
        return total

    def data_copy(block, target, sems):
        return (
            pltpu.make_async_remote_copy(
                src_ref=data.at[block], dst_ref=data.at[block],
                send_sem=sems.at[0], recv_sem=recv_sem.at[block, 0],
                device_id=(dp, target), device_id_type=MESH),
            pltpu.make_async_remote_copy(
                src_ref=meta.at[block], dst_ref=meta.at[block],
                send_sem=sems.at[1], recv_sem=recv_sem.at[block, 1],
                device_id=(dp, target), device_id_type=MESH),
        )

    def ship(block, target, sems):
        for copy in data_copy(block, target, sems):
            copy.start()

    def sent(block, target, sems):
        for copy in data_copy(block, target, sems):
            copy.wait_send()

    def arrived(block):
        for copy in data_copy(block, sib, own_send.at[0]):
            copy.wait_recv()

    own_rows_in = pl.ds(pl.multiple_of(dp * half_in, 16), half_in)
    own_rows_dn = pl.ds(pl.multiple_of(dp * half_dn, 16), half_dn)
    peer_rows_dn = pl.ds(pl.multiple_of((1 - dp) * half_dn, 16), half_dn)
    local = [
        pltpu.make_async_copy(tok_in, data.at[me, 0], local_sem.at[0]),
        pltpu.make_async_copy(grad_in, data.at[me, 1], local_sem.at[1]),
        pltpu.make_async_copy(win_in, win.at[own_rows_in], local_sem.at[2]),
        pltpu.make_async_copy(wdn_in, wdn.at[own_rows_dn], local_sem.at[3]),
    ]
    for copy in local:
        copy.start()

    barrier = pltpu.get_barrier_semaphore()
    partners = [(dp, sib), (dp, y_peer), (1 - dp, me)]
    for step in range(1, depth):
        partners.append((dp, block_of((z + step) % depth, y, c)))
    for partner in partners:
        pl.semaphore_signal(barrier, inc=1, device_id=partner, device_id_type=MESH)

    experts = lax.broadcasted_iota(jnp.int32, (expert_count, token_rows), 0)
    marks = jnp.zeros((expert_count, token_rows), F32)
    scale = jnp.zeros((expert_count, token_rows), F32)
    for k in range(ids_ref.shape[0]):
        hit = ids_ref[k : k + 1, :] == experts
        marks = marks + jnp.where(hit, 1.0, 0.0)
        scale = scale + jnp.where(hit, gates_ref[k : k + 1, :], 0.0)
    before = (
        lax.broadcasted_iota(jnp.int32, (token_rows, token_rows), 0)
        < lax.broadcasted_iota(jnp.int32, (token_rows, token_rows), 1)
    )
    ranks = jnp.dot(
        marks.astype(BF16), jnp.where(before, 1.0, 0.0).astype(BF16), preferred_element_type=F32
    )
    meta[me, 0:expert_count, :] = jnp.where(marks > 0.5, ranks, -1.0)
    meta[me, expert_count : 2 * expert_count, :] = scale

    pl.semaphore_wait(barrier, len(partners))

    weights = [
        pltpu.make_async_remote_copy(
            src_ref=src, dst_ref=dst, send_sem=w_send.at[i], recv_sem=w_recv.at[i],
            device_id=(1 - dp, me), device_id_type=MESH)
        for i, (src, dst) in enumerate(
            ((win_in, win.at[own_rows_in]), (wdn_in, wdn.at[own_rows_dn])))
    ]
    local[0].wait()
    local[1].wait()

    @pl.when(z > 0)
    def _():
        ship(me, block_of(jnp.maximum(z - 1, 0), y, c), own_send.at[0])

    @pl.when(z < depth - 1)
    def _():
        ship(me, block_of(jnp.minimum(z + 1, depth - 1), y, c), own_send.at[1])

    ship(me, y_peer, y_send.at[0])
    for copy in weights:
        copy.start()
    ship(me, sib, sib_send.at[0, 0])

    def onward(zz):
        step_to = jnp.where(zz < z, z + 1, z - 1)
        return (step_to >= 0) & (step_to < depth), jnp.clip(step_to, 0, depth - 1)

    def arrivals(k):
        zz = near(k)
        block = block_of(zz, y, c)
        arrived(block)
        more, step_to = onward(zz)

        @pl.when(more)
        def _():
            ship(block, block_of(step_to, y, c), fwd_send.at[k])

        ship(block, y_peer, y_send.at[k])
        ship(block, sib, sib_send.at[k, 0])

    def sib_part(k):
        return pltpu.make_async_remote_copy(
            src_ref=part.at[k, 1 - c], dst_ref=sib_in.at[k],
            send_sem=sib_part_send.at[k], recv_sem=sib_part_recv.at[k],
            device_id=(dp, sib), device_id_type=MESH)

    def y_part(k):
        return pltpu.make_async_remote_copy(
            src_ref=y_out.at[k], dst_ref=y_in.at[k],
            send_sem=y_part_send.at[k], recv_sem=y_part_recv.at[k],
            device_id=(dp, y_peer), device_id_type=MESH)

    def z_part(k, slot):
        return pltpu.make_async_remote_copy(
            src_ref=z_out.at[k], dst_ref=z_in.at[slot],
            send_sem=z_part_send.at[k], recv_sem=z_part_recv.at[slot],
            device_id=(dp, block_of(near(k), y, c)), device_id_type=MESH)

    def gin_part(i):
        rows = pl.ds(pl.multiple_of(i * tile, tile), tile)
        return pltpu.make_async_remote_copy(
            src_ref=gin_send.at[rows], dst_ref=gin_recv.at[rows],
            send_sem=g_send.at[i], recv_sem=g_recv.at[i],
            device_id=(1 - dp, me), device_id_type=MESH)

    half_tiles = half_in // tile
    keep = pltpu.make_async_copy(z_out.at[0], z_in.at[z], local_sem.at[4])

    def grad_in_rows(half, i):
        columns = pl.ds(pl.multiple_of(half * half_in + i * tile, tile), tile)
        return contract_first(xs[:, columns], dpre[...]).astype(BF16)

    gdn_part = pltpu.make_async_remote_copy(
        src_ref=gdn_send, dst_ref=gdn_recv,
        send_sem=g_send.at[half_tiles], recv_sem=g_recv.at[half_tiles],
        device_id=(1 - dp, me), device_id_type=MESH)

    def combine_y(k):
        sib_part(k).wait_recv()
        y_out[k] = (
            part[k, c, 1 - y].astype(F32) + sib_in[k, 1 - y].astype(F32)
        ).astype(BF16)
        y_part(k).start()

    def combine_z(k):
        y_part(k).wait_recv()
        z_out[k] = (
            part[k, c, y].astype(F32) + sib_in[k, y].astype(F32) + y_in[k].astype(F32)
        ).astype(BF16)

        if k > 0:
            z_part(k, z).start()
        else:
            keep.start()

    for k in range(1, min(3, depth)):
        arrivals(k)
    local[2].wait()
    local[3].wait()

    def chunk(k, carry):
        zz = near(k)
        block = block_of(zz, 1 - y, c)
        arrived(block)
        ship(block, sib, sib_send.at[k, 1])
        arrived(block_of(zz, y, 1 - c))
        arrived(block_of(zz, 1 - y, 1 - c))

        @pl.when(k == 0)
        def _():
            for copy in weights:
                copy.wait_recv()

        last = k == depth - 1

        @pl.when(last)
        def _():
            for early in range(depth - 2):
                combine_y(early)

        first = zz * 4
        at_rows = pl.ds(pl.multiple_of(k * slots, 16), slots)
        slot_rows = lax.broadcasted_iota(jnp.int32, (slots, token_rows), 0)
        slot_gate = jnp.zeros((slots, 1), F32)
        for j in range(4):
            rank = meta[first + j, pl.ds(me, 1), :].astype(jnp.int32)
            place = jnp.where(rank >= 0, rank + j * capacity, -1)
            scale_row = meta[first + j, pl.ds(expert_count + me, 1), :]
            hit = slot_rows == place
            slot_gate = slot_gate + jnp.sum(
                jnp.where(hit, scale_row, 0.0), axis=1, keepdims=True
            )
            sel[:, j * token_rows : (j + 1) * token_rows] = jnp.where(hit, 1.0, 0.0).astype(BF16)
        chosen = sel[...]
        chunk_tokens = data[pl.ds(first, 4), 0].reshape(4 * token_rows, model_width)
        own_tokens = jnp.dot(chosen, chunk_tokens, preferred_element_type=F32).astype(BF16)
        xs[at_rows, :] = own_tokens
        chunk_grads = data[pl.ds(first, 4), 1].reshape(4 * token_rows, model_width)
        own_grads = (
            slot_gate * jnp.dot(chosen, chunk_grads, preferred_element_type=F32)
        ).astype(BF16)
        gs[at_rows, :] = own_grads
        preact = jnp.dot(xs[at_rows, :], win[...], preferred_element_type=F32)
        grad_hidden = contract_last(gs[at_rows, :], wdn[...])
        act[at_rows, :] = hidden_from(preact)
        dpre[at_rows, :] = pre_grads(preact, grad_hidden)

        @pl.when((k >= 1) & (k + 2 < depth))
        def _():
            arrivals(jnp.minimum(k + 2, depth - 1))

        @pl.when(last)
        def _():
            @pl.loop(0, half_tiles)
            def _(i):
                gin_send[pl.ds(pl.multiple_of(i * tile, tile), tile), :] = grad_in_rows(1 - dp, i)
                gin_part(i).start()

            acc_dn[...] = contract_first(act[...], gs[...])
            gdn_send[...] = acc_dn[peer_rows_dn, :].astype(BF16)
            gdn_part.start()

        back = contract_last(dpre[at_rows, :], win[...]).astype(BF16)
        spread = contract_first(sel[...], back).astype(BF16)
        for j in range(4):
            part[k, j % 2, j // 2] = spread[j * token_rows : (j + 1) * token_rows]
        sib_part(k).start()
        return carry

    lax.fori_loop(0, depth, chunk, 0)
    combine_y(depth - 2)
    combine_y(depth - 1)

    @pl.loop(0, half_tiles)
    def _(i):
        gin_own[pl.ds(pl.multiple_of(i * tile, tile), tile), :] = grad_in_rows(dp, i)

    gdn_own[...] = acc_dn[own_rows_dn, :].astype(BF16)
    for k in range(depth):
        combine_z(k)
    for step in range(1, depth):
        z_part(step, (z + step) % depth).wait_recv()
    keep.wait()
    for i in range(half_tiles):
        gin_part(i).wait_recv()
    gdn_part.wait_recv()

    @pl.when(z > 0)
    def _():
        sent(me, sib, own_send.at[0])

    @pl.when(z < depth - 1)
    def _():
        sent(me, sib, own_send.at[1])

    for k in range(depth):
        sent(me, y_peer, y_send.at[k])
        sent(me, sib, sib_send.at[k, 0])
        sent(me, sib, sib_send.at[k, 1])
        sib_part(k).wait_send()
        y_part(k).wait_send()
        if k > 0:
            more, _ = onward(near(k))

            @pl.when(more)
            def _():
                sent(me, sib, fwd_send.at[k])

            z_part(k, z).wait_send()
    for copy in weights:
        copy.wait_send()
    for i in range(half_tiles):
        gin_part(i).wait_send()
    gdn_part.wait_send()


def fused_on_device(tokens, grad_out, expert_ids, gates, w_in, w_down):
    token_rows, model_width = tokens.shape
    route_total = token_rows * expert_ids.shape[1]
    expert_count = lax.axis_size("expert")
    capacity = route_total // expert_count + max(1, route_total // (8 * expert_count))
    depth = expert_count // 4
    slots = 4 * capacity
    half_in, in_width = w_in.shape[1:]
    half_dn = w_down.shape[1]
    half_tiles = half_in // (model_width // 4)
    dma = lambda *shape: pltpu.SemaphoreType.DMA(shape)
    vmem = lambda shape, dtype=BF16: pltpu.VMEM(shape, dtype)
    z_parts, own_in, other_in, own_dn, other_dn = pl.pallas_call(
        functools.partial(fused_kernel, expert_count, capacity),
        out_shape=(
            jax.ShapeDtypeStruct((depth, token_rows, model_width), BF16),
            jax.ShapeDtypeStruct((half_in, in_width), BF16),
            jax.ShapeDtypeStruct((half_in, in_width), BF16),
            jax.ShapeDtypeStruct((half_dn, model_width), BF16),
            jax.ShapeDtypeStruct((half_dn, model_width), BF16),
        ),
        in_specs=[pl.BlockSpec(memory_space=pltpu.VMEM)] * 2
        + [pl.BlockSpec(memory_space=pl.ANY)] * 4,
        out_specs=(
            pl.BlockSpec(memory_space=pl.ANY),
            pl.BlockSpec(memory_space=pltpu.VMEM),
            pl.BlockSpec(memory_space=pl.ANY),
            pl.BlockSpec(memory_space=pltpu.VMEM),
            pl.BlockSpec(memory_space=pl.ANY),
        ),
        scratch_shapes=[
            vmem((expert_count, 2, token_rows, model_width)),
            vmem((expert_count, 2 * expert_count, token_rows), F32),
            vmem((2 * half_in, in_width)),
            vmem((2 * half_dn, model_width)),
            vmem((2 * half_dn, model_width), F32),
            vmem((slots, 4 * token_rows)),
            vmem((depth * slots, model_width)),
            vmem((depth * slots, model_width)),
            vmem((depth * slots, in_width // 2)),
            vmem((depth * slots, in_width)),
            vmem((depth, 2, 2, token_rows, model_width)),
            vmem((depth, 2, token_rows, model_width)),
            vmem((depth, token_rows, model_width)),
            vmem((depth, token_rows, model_width)),
            vmem((depth, token_rows, model_width)),
            vmem((half_in, in_width)),
            vmem((half_dn, model_width)),
            dma(5), dma(2, 2), dma(depth, 2), dma(depth, 2), dma(depth, 2, 2),
            dma(expert_count, 2), dma(2), dma(2), dma(depth), dma(depth), dma(depth), dma(depth),
            dma(depth), dma(depth), dma(half_tiles + 1), dma(half_tiles + 1),
        ],
        compiler_params=pltpu.CompilerParams(
            collective_id=0, has_side_effects=True, vmem_limit_bytes=VMEM_BYTES
        ),
    )(expert_ids.T, gates.T, tokens, grad_out, w_in[0], w_down[0])
    grad_tokens = jnp.sum(z_parts.astype(F32), axis=0).astype(BF16)
    grad_in = own_in.astype(F32) + other_in.astype(F32)
    grad_down = own_dn.astype(F32) + other_dn.astype(F32)
    return grad_tokens, grad_in[None], grad_down[None]


def fits_fused(mesh):
    return mesh.shape["dp"] == 2 and mesh.shape["expert"] in (8, 16)


def solution(mesh):
    in_specs = (
        P(("dp", "expert"), None),
        P(("dp", "expert"), None),
        P(("dp", "expert"), None),
        P(("dp", "expert"), None),
        P("expert", "dp", None),
        P("expert", "dp", None),
    )
    out_specs = (P(("dp", "expert"), None), P("expert", "dp", None), P("expert", "dp", None))
    return jax.shard_map(
        fused_on_device if fits_fused(mesh) else on_device,
        mesh=mesh, in_specs=in_specs, out_specs=out_specs, check_vma=False
    )
```

```python
import functools

import jax
import jax.numpy as jnp
from jax import lax
from jax.experimental import pallas as pl
from jax.experimental.pallas import tpu as pltpu
from jax.sharding import PartitionSpec as P

MESH = pl.DeviceIdType.MESH
F32 = jnp.float32
BF16 = jnp.bfloat16
VMEM_BYTES = 56 * 1024 * 1024


def hidden_from(preact):
    half_width = preact.shape[1] // 2
    gate_pre = preact[:, :half_width]
    up_pre = preact[:, half_width:]
    sigmoid_gate = jax.nn.sigmoid(gate_pre)
    return (gate_pre * sigmoid_gate * up_pre).astype(jnp.bfloat16)


def pre_grads(preact, grad_hidden):
    half_width = preact.shape[1] // 2
    gate_pre = preact[:, :half_width]
    up_pre = preact[:, half_width:]
    sigmoid_gate = jax.nn.sigmoid(gate_pre)
    grad_gate = grad_hidden * up_pre * sigmoid_gate * (1.0 + gate_pre * (1.0 - sigmoid_gate))
    grad_up = grad_hidden * gate_pre * sigmoid_gate
    return jnp.concatenate([grad_gate, grad_up], axis=1).astype(jnp.bfloat16)


def contract_first(left, right):
    return lax.dot_general(
        left, right, (((0,), (0,)), ((), ())), preferred_element_type=jnp.float32
    )


def contract_last(left, right):
    return lax.dot_general(
        left, right, (((1,), (1,)), ((), ())), preferred_element_type=jnp.float32
    )


def on_device(tokens, grad_out, expert_ids, gates, w_in, w_down):
    token_rows, model_width = tokens.shape
    route_width = expert_ids.shape[1]
    expert_count = lax.axis_size("expert")
    route_total = token_rows * route_width
    capacity = route_total // expert_count + max(1, route_total // (8 * expert_count))
    slot_total = expert_count * capacity
    flat_ids = expert_ids.reshape(route_total)
    route_marks = (flat_ids[:, None] == jnp.arange(expert_count, dtype=jnp.int32)[None, :]).astype(
        jnp.int32
    )
    route_index = jnp.arange(route_total, dtype=jnp.int32)
    lower_table = (route_index[None, :] <= route_index[:, None]).astype(jnp.bfloat16)
    running = jnp.dot(
        lower_table, route_marks.astype(jnp.bfloat16), preferred_element_type=jnp.float32
    )
    slot_ranks = jnp.sum((running.astype(jnp.int32) - 1) * route_marks, axis=1)
    targets = flat_ids * capacity + slot_ranks
    route_of_slot = jnp.full((slot_total,), route_total, jnp.int32).at[targets].set(route_index)
    occupied = route_of_slot < route_total
    clipped = jnp.minimum(route_of_slot, route_total - 1)
    source_rows = clipped // route_width
    slot_gates = jnp.where(
        occupied, gates.reshape(route_total)[clipped], jnp.zeros((), jnp.float32)
    )
    send_tokens = jnp.where(occupied[:, None], tokens[source_rows], jnp.zeros((), jnp.bfloat16))
    send_grads = (slot_gates[:, None] * grad_out[source_rows].astype(jnp.float32)).astype(
        jnp.bfloat16
    )
    recv_tokens, recv_grads = (
        lax.all_to_all(
            send_tokens.reshape(expert_count, capacity, model_width),
            "expert",
            split_axis=0,
            concat_axis=0,
            tiled=True,
        ),
        lax.all_to_all(
            send_grads.reshape(expert_count, capacity, model_width),
            "expert",
            split_axis=0,
            concat_axis=0,
            tiled=True,
        ),
    )
    slot_tokens = recv_tokens.reshape(slot_total, model_width)
    slot_grads = recv_grads.reshape(slot_total, model_width)
    local_in = w_in[0]
    local_down = w_down[0]
    full_in, full_down = (
        lax.all_gather(local_in, "dp", axis=0, tiled=True),
        lax.all_gather(local_down, "dp", axis=0, tiled=True),
    )
    preact = jnp.dot(slot_tokens, full_in, preferred_element_type=jnp.float32)
    grad_hidden = contract_last(slot_grads, full_down)
    pre_grad = pre_grads(preact, grad_hidden)
    slot_back = contract_last(pre_grad, full_in).astype(jnp.bfloat16)
    hidden_act = hidden_from(preact)
    columns = slot_tokens
    grad_in_local = lax.psum_scatter(
        contract_first(columns, pre_grad).astype(jnp.bfloat16),
        "dp",
        scatter_dimension=0,
        tiled=True,
    ).astype(jnp.float32)
    columns = hidden_act
    grad_down_local = lax.psum_scatter(
        contract_first(columns, slot_grads).astype(jnp.bfloat16),
        "dp",
        scatter_dimension=0,
        tiled=True,
    ).astype(jnp.float32)
    slot_return = lax.all_to_all(
        slot_back.reshape(expert_count, capacity, model_width),
        "expert",
        split_axis=0,
        concat_axis=0,
        tiled=True,
    )
    per_route = slot_return.reshape(slot_total, model_width)[targets]
    grad_tokens = jnp.sum(
        per_route.reshape(token_rows, route_width, model_width).astype(jnp.float32), axis=1
    ).astype(jnp.bfloat16)
    return (grad_tokens, grad_in_local[None], grad_down_local[None])


def fused_kernel(
    expert_count, capacity,
    ids_ref, gates_ref, tok_in, grad_in, win_in, wdn_in,
    z_in, gin_own, gin_recv, gdn_own, gdn_recv,
    data, meta, win, wdn, acc_dn, sel, xs, gs, act, dpre, part,
    sib_in, y_out, y_in, z_out, gin_send, gdn_send,
    local_sem, own_send, fwd_send, y_send, sib_send, recv_sem,
    w_send, w_recv, sib_part_send, sib_part_recv, y_part_send, y_part_recv,
    z_part_send, z_part_recv, g_send, g_recv,
):
    depth = expert_count // 4
    dp = lax.axis_index("dp")
    me = lax.axis_index("expert")
    z, y, c = me // 4, (me // 2) % 2, me % 2
    token_rows, model_width = tok_in.shape
    half_in, half_dn = win_in.shape[0], wdn_in.shape[0]
    half_width = wdn.shape[0]
    slots = 4 * capacity
    tile = model_width // 4

    def block_of(zz, yy, cc):
        return zz * 4 + yy * 2 + cc

    sib, y_peer = block_of(z, y, 1 - c), block_of(z, 1 - y, c)
    table = [sorted(range(depth), key=lambda b: (abs(b - zz), b)) for zz in range(depth)]

    def near(k):
        total = jnp.int32(0)
        for zz in range(depth):
            for kk in range(depth):
                hit = (z == zz).astype(jnp.int32) * (jnp.int32(k) == kk).astype(jnp.int32)
                total = total + hit * table[zz][kk]
        return total

    def data_copy(block, target, sems):
        return (
            pltpu.make_async_remote_copy(
                src_ref=data.at[block], dst_ref=data.at[block],
                send_sem=sems.at[0], recv_sem=recv_sem.at[block, 0],
                device_id=(dp, target), device_id_type=MESH),
            pltpu.make_async_remote_copy(
                src_ref=meta.at[block], dst_ref=meta.at[block],
                send_sem=sems.at[1], recv_sem=recv_sem.at[block, 1],
                device_id=(dp, target), device_id_type=MESH),
        )

    def ship(block, target, sems):
        for copy in data_copy(block, target, sems):
            copy.start()

    def sent(block, target, sems):
        for copy in data_copy(block, target, sems):
            copy.wait_send()

    def arrived(block):
        for copy in data_copy(block, sib, own_send.at[0]):
            copy.wait_recv()

    own_rows_in = pl.ds(pl.multiple_of(dp * half_in, 16), half_in)
    own_rows_dn = pl.ds(pl.multiple_of(dp * half_dn, 16), half_dn)
    peer_rows_dn = pl.ds(pl.multiple_of((1 - dp) * half_dn, 16), half_dn)
    local = [
        pltpu.make_async_copy(tok_in, data.at[me, 0], local_sem.at[0]),
        pltpu.make_async_copy(grad_in, data.at[me, 1], local_sem.at[1]),
        pltpu.make_async_copy(win_in, win.at[own_rows_in], local_sem.at[2]),
        pltpu.make_async_copy(wdn_in, wdn.at[own_rows_dn], local_sem.at[3]),
    ]
    for copy in local:
        copy.start()

    barrier = pltpu.get_barrier_semaphore()
    partners = [(dp, sib), (dp, y_peer), (1 - dp, me)]
    for step in range(1, depth):
        partners.append((dp, block_of((z + step) % depth, y, c)))
    for partner in partners:
        pl.semaphore_signal(barrier, inc=1, device_id=partner, device_id_type=MESH)

    experts = lax.broadcasted_iota(jnp.int32, (expert_count, token_rows), 0)
    marks = jnp.zeros((expert_count, token_rows), F32)
    scale = jnp.zeros((expert_count, token_rows), F32)
    for k in range(ids_ref.shape[0]):
        hit = ids_ref[k : k + 1, :] == experts
        marks = marks + jnp.where(hit, 1.0, 0.0)
        scale = scale + jnp.where(hit, gates_ref[k : k + 1, :], 0.0)
    before = (
        lax.broadcasted_iota(jnp.int32, (token_rows, token_rows), 0)
        < lax.broadcasted_iota(jnp.int32, (token_rows, token_rows), 1)
    )
    ranks = jnp.dot(
        marks.astype(BF16), jnp.where(before, 1.0, 0.0).astype(BF16), preferred_element_type=F32
    )
    meta[me, 0:expert_count, :] = jnp.where(marks > 0.5, ranks, -1.0)
    meta[me, expert_count : 2 * expert_count, :] = scale

    pl.semaphore_wait(barrier, len(partners))

    weights = [
        pltpu.make_async_remote_copy(
            src_ref=src, dst_ref=dst, send_sem=w_send.at[i], recv_sem=w_recv.at[i],
            device_id=(1 - dp, me), device_id_type=MESH)
        for i, (src, dst) in enumerate(
            ((win_in, win.at[own_rows_in]), (wdn_in, wdn.at[own_rows_dn])))
    ]
    local[0].wait()
    local[1].wait()

    @pl.when(z > 0)
    def _():
        ship(me, block_of(jnp.maximum(z - 1, 0), y, c), own_send.at[0])

    @pl.when(z < depth - 1)
    def _():
        ship(me, block_of(jnp.minimum(z + 1, depth - 1), y, c), own_send.at[1])

    ship(me, y_peer, y_send.at[0])
    for copy in weights:
        copy.start()
    ship(me, sib, sib_send.at[0, 0])

    def onward(zz):
        step_to = jnp.where(zz < z, z + 1, z - 1)
        return (step_to >= 0) & (step_to < depth), jnp.clip(step_to, 0, depth - 1)

    def arrivals(k):
        zz = near(k)
        block = block_of(zz, y, c)
        arrived(block)
        more, step_to = onward(zz)

        @pl.when(more)
        def _():
            ship(block, block_of(step_to, y, c), fwd_send.at[k])

        ship(block, y_peer, y_send.at[k])
        ship(block, sib, sib_send.at[k, 0])

    def sib_part(k):
        return pltpu.make_async_remote_copy(
            src_ref=part.at[k, 1 - c], dst_ref=sib_in.at[k],
            send_sem=sib_part_send.at[k], recv_sem=sib_part_recv.at[k],
            device_id=(dp, sib), device_id_type=MESH)

    def y_part(k):
        return pltpu.make_async_remote_copy(
            src_ref=y_out.at[k], dst_ref=y_in.at[k],
            send_sem=y_part_send.at[k], recv_sem=y_part_recv.at[k],
            device_id=(dp, y_peer), device_id_type=MESH)

    def z_part(k, slot):
        return pltpu.make_async_remote_copy(
            src_ref=z_out.at[k], dst_ref=z_in.at[slot],
            send_sem=z_part_send.at[k], recv_sem=z_part_recv.at[slot],
            device_id=(dp, block_of(near(k), y, c)), device_id_type=MESH)

    def gin_part(i):
        rows = pl.ds(pl.multiple_of(i * tile, tile), tile)
        return pltpu.make_async_remote_copy(
            src_ref=gin_send.at[rows], dst_ref=gin_recv.at[rows],
            send_sem=g_send.at[i], recv_sem=g_recv.at[i],
            device_id=(1 - dp, me), device_id_type=MESH)

    half_tiles = half_in // tile
    keep = pltpu.make_async_copy(z_out.at[0], z_in.at[z], local_sem.at[4])

    def grad_in_rows(half, i):
        columns = pl.ds(pl.multiple_of(half * half_in + i * tile, tile), tile)
        return contract_first(xs[:, columns], dpre[...]).astype(BF16)

    gdn_part = pltpu.make_async_remote_copy(
        src_ref=gdn_send, dst_ref=gdn_recv,
        send_sem=g_send.at[half_tiles], recv_sem=g_recv.at[half_tiles],
        device_id=(1 - dp, me), device_id_type=MESH)

    def combine_y(k):
        sib_part(k).wait_recv()
        y_out[k] = (
            part[k, c, 1 - y].astype(F32) + sib_in[k, 1 - y].astype(F32)
        ).astype(BF16)
        y_part(k).start()

    def combine_z(k):
        y_part(k).wait_recv()
        z_out[k] = (
            part[k, c, y].astype(F32) + sib_in[k, y].astype(F32) + y_in[k].astype(F32)
        ).astype(BF16)

        if k > 0:
            z_part(k, z).start()
        else:
            keep.start()

    for k in range(1, min(3, depth)):
        arrivals(k)
    local[2].wait()
    local[3].wait()

    def chunk(k, carry):
        zz = near(k)
        block = block_of(zz, 1 - y, c)
        arrived(block)
        ship(block, sib, sib_send.at[k, 1])
        arrived(block_of(zz, y, 1 - c))
        arrived(block_of(zz, 1 - y, 1 - c))

        @pl.when(k == 0)
        def _():
            for copy in weights:
                copy.wait_recv()

        last = k == depth - 1

        @pl.when(last)
        def _():
            for early in range(1, depth - 1):
                combine_y(early)

        first = zz * 4
        at_rows = pl.ds(pl.multiple_of(k * slots, 16), slots)
        slot_rows = lax.broadcasted_iota(jnp.int32, (slots, token_rows), 0)
        slot_gate = jnp.zeros((slots, 1), F32)
        for j in range(4):
            rank = meta[first + j, pl.ds(me, 1), :].astype(jnp.int32)
            place = jnp.where(rank >= 0, rank + j * capacity, -1)
            scale_row = meta[first + j, pl.ds(expert_count + me, 1), :]
            hit = slot_rows == place
            slot_gate = slot_gate + jnp.sum(
                jnp.where(hit, scale_row, 0.0), axis=1, keepdims=True
            )
            sel[:, j * token_rows : (j + 1) * token_rows] = jnp.where(hit, 1.0, 0.0).astype(BF16)
        chosen = sel[...]
        chunk_tokens = data[pl.ds(first, 4), 0].reshape(4 * token_rows, model_width)
        own_tokens = jnp.dot(chosen, chunk_tokens, preferred_element_type=F32).astype(BF16)
        xs[at_rows, :] = own_tokens
        chunk_grads = data[pl.ds(first, 4), 1].reshape(4 * token_rows, model_width)
        own_grads = (
            slot_gate * jnp.dot(chosen, chunk_grads, preferred_element_type=F32)
        ).astype(BF16)
        gs[at_rows, :] = own_grads
        preact = jnp.dot(xs[at_rows, :], win[...], preferred_element_type=F32)
        grad_hidden = contract_last(gs[at_rows, :], wdn[...])
        act[at_rows, :] = hidden_from(preact)
        dpre[at_rows, :] = pre_grads(preact, grad_hidden)

        @pl.when((k >= 1) & (k + 2 < depth))
        def _():
            arrivals(jnp.minimum(k + 2, depth - 1))

        @pl.when(last)
        def _():
            @pl.loop(0, half_tiles)
            def _(i):
                gin_send[pl.ds(pl.multiple_of(i * tile, tile), tile), :] = grad_in_rows(1 - dp, i)
                gin_part(i).start()

            acc_dn[...] = contract_first(act[...], gs[...])
            gdn_send[...] = acc_dn[peer_rows_dn, :].astype(BF16)
            gdn_part.start()

        back = contract_last(dpre[at_rows, :], win[...]).astype(BF16)
        spread = contract_first(sel[...], back).astype(BF16)
        for j in range(4):
            part[k, j % 2, j // 2] = spread[j * token_rows : (j + 1) * token_rows]
        sib_part(k).start()
        return carry

    lax.fori_loop(0, depth, chunk, 0)
    combine_y(depth - 1)
    for k in range(1, depth - 1):
        combine_z(k)
    combine_y(0)

    @pl.loop(0, half_tiles)
    def _(i):
        gin_own[pl.ds(pl.multiple_of(i * tile, tile), tile), :] = grad_in_rows(dp, i)

    combine_z(depth - 1)
    gdn_own[...] = acc_dn[own_rows_dn, :].astype(BF16)
    combine_z(0)
    for step in range(1, depth):
        z_part(step, (z + step) % depth).wait_recv()
    keep.wait()
    for i in range(half_tiles):
        gin_part(i).wait_recv()
    gdn_part.wait_recv()

    @pl.when(z > 0)
    def _():
        sent(me, sib, own_send.at[0])

    @pl.when(z < depth - 1)
    def _():
        sent(me, sib, own_send.at[1])

    for k in range(depth):
        sent(me, y_peer, y_send.at[k])
        sent(me, sib, sib_send.at[k, 0])
        sent(me, sib, sib_send.at[k, 1])
        sib_part(k).wait_send()
        y_part(k).wait_send()
        if k > 0:
            more, _ = onward(near(k))

            @pl.when(more)
            def _():
                sent(me, sib, fwd_send.at[k])

            z_part(k, z).wait_send()
    for copy in weights:
        copy.wait_send()
    for i in range(half_tiles):
        gin_part(i).wait_send()
    gdn_part.wait_send()


def fused_on_device(tokens, grad_out, expert_ids, gates, w_in, w_down):
    token_rows, model_width = tokens.shape
    route_total = token_rows * expert_ids.shape[1]
    expert_count = lax.axis_size("expert")
    capacity = route_total // expert_count + max(1, route_total // (8 * expert_count))
    depth = expert_count // 4
    slots = 4 * capacity
    half_in, in_width = w_in.shape[1:]
    half_dn = w_down.shape[1]
    half_tiles = half_in // (model_width // 4)
    dma = lambda *shape: pltpu.SemaphoreType.DMA(shape)
    vmem = lambda shape, dtype=BF16: pltpu.VMEM(shape, dtype)
    z_parts, own_in, other_in, own_dn, other_dn = pl.pallas_call(
        functools.partial(fused_kernel, expert_count, capacity),
        out_shape=(
            jax.ShapeDtypeStruct((depth, token_rows, model_width), BF16),
            jax.ShapeDtypeStruct((half_in, in_width), BF16),
            jax.ShapeDtypeStruct((half_in, in_width), BF16),
            jax.ShapeDtypeStruct((half_dn, model_width), BF16),
            jax.ShapeDtypeStruct((half_dn, model_width), BF16),
        ),
        in_specs=[pl.BlockSpec(memory_space=pltpu.VMEM)] * 2
        + [pl.BlockSpec(memory_space=pl.ANY)] * 4,
        out_specs=(
            pl.BlockSpec(memory_space=pl.ANY),
            pl.BlockSpec(memory_space=pltpu.VMEM),
            pl.BlockSpec(memory_space=pl.ANY),
            pl.BlockSpec(memory_space=pltpu.VMEM),
            pl.BlockSpec(memory_space=pl.ANY),
        ),
        scratch_shapes=[
            vmem((expert_count, 2, token_rows, model_width)),
            vmem((expert_count, 2 * expert_count, token_rows), F32),
            vmem((2 * half_in, in_width)),
            vmem((2 * half_dn, model_width)),
            vmem((2 * half_dn, model_width), F32),
            vmem((slots, 4 * token_rows)),
            vmem((depth * slots, model_width)),
            vmem((depth * slots, model_width)),
            vmem((depth * slots, in_width // 2)),
            vmem((depth * slots, in_width)),
            vmem((depth, 2, 2, token_rows, model_width)),
            vmem((depth, 2, token_rows, model_width)),
            vmem((depth, token_rows, model_width)),
            vmem((depth, token_rows, model_width)),
            vmem((depth, token_rows, model_width)),
            vmem((half_in, in_width)),
            vmem((half_dn, model_width)),
            dma(5), dma(2, 2), dma(depth, 2), dma(depth, 2), dma(depth, 2, 2),
            dma(expert_count, 2), dma(2), dma(2), dma(depth), dma(depth), dma(depth), dma(depth),
            dma(depth), dma(depth), dma(half_tiles + 1), dma(half_tiles + 1),
        ],
        compiler_params=pltpu.CompilerParams(
            collective_id=0, has_side_effects=True, vmem_limit_bytes=VMEM_BYTES
        ),
    )(expert_ids.T, gates.T, tokens, grad_out, w_in[0], w_down[0])
    grad_tokens = jnp.sum(z_parts.astype(F32), axis=0).astype(BF16)
    grad_in = own_in.astype(F32) + other_in.astype(F32)
    grad_down = own_dn.astype(F32) + other_dn.astype(F32)
    return grad_tokens, grad_in[None], grad_down[None]


def fits_fused(mesh):
    return mesh.shape["dp"] == 2 and mesh.shape["expert"] in (8, 16)


def solution(mesh):
    in_specs = (
        P(("dp", "expert"), None),
        P(("dp", "expert"), None),
        P(("dp", "expert"), None),
        P(("dp", "expert"), None),
        P("expert", "dp", None),
        P("expert", "dp", None),
    )
    out_specs = (P(("dp", "expert"), None), P("expert", "dp", None), P("expert", "dp", None))
    return jax.shard_map(
        fused_on_device if fits_fused(mesh) else on_device,
        mesh=mesh, in_specs=in_specs, out_specs=out_specs, check_vma=False
    )
```

```python
import functools

import jax
import jax.numpy as jnp
from jax import lax
from jax.experimental import pallas as pl
from jax.experimental.pallas import tpu as pltpu
from jax.sharding import PartitionSpec as P

MESH = pl.DeviceIdType.MESH
F32 = jnp.float32
BF16 = jnp.bfloat16
VMEM_BYTES = 56 * 1024 * 1024


def hidden_from(preact):
    half_width = preact.shape[1] // 2
    gate_pre = preact[:, :half_width]
    up_pre = preact[:, half_width:]
    sigmoid_gate = jax.nn.sigmoid(gate_pre)
    return (gate_pre * sigmoid_gate * up_pre).astype(jnp.bfloat16)


def pre_grads(preact, grad_hidden):
    half_width = preact.shape[1] // 2
    gate_pre = preact[:, :half_width]
    up_pre = preact[:, half_width:]
    sigmoid_gate = jax.nn.sigmoid(gate_pre)
    grad_gate = grad_hidden * up_pre * sigmoid_gate * (1.0 + gate_pre * (1.0 - sigmoid_gate))
    grad_up = grad_hidden * gate_pre * sigmoid_gate
    return jnp.concatenate([grad_gate, grad_up], axis=1).astype(jnp.bfloat16)


def contract_first(left, right):
    return lax.dot_general(
        left, right, (((0,), (0,)), ((), ())), preferred_element_type=jnp.float32
    )


def contract_last(left, right):
    return lax.dot_general(
        left, right, (((1,), (1,)), ((), ())), preferred_element_type=jnp.float32
    )


def on_device(tokens, grad_out, expert_ids, gates, w_in, w_down):
    token_rows, model_width = tokens.shape
    route_width = expert_ids.shape[1]
    expert_count = lax.axis_size("expert")
    route_total = token_rows * route_width
    capacity = route_total // expert_count + max(1, route_total // (8 * expert_count))
    slot_total = expert_count * capacity
    flat_ids = expert_ids.reshape(route_total)
    route_marks = (flat_ids[:, None] == jnp.arange(expert_count, dtype=jnp.int32)[None, :]).astype(
        jnp.int32
    )
    route_index = jnp.arange(route_total, dtype=jnp.int32)
    lower_table = (route_index[None, :] <= route_index[:, None]).astype(jnp.bfloat16)
    running = jnp.dot(
        lower_table, route_marks.astype(jnp.bfloat16), preferred_element_type=jnp.float32
    )
    slot_ranks = jnp.sum((running.astype(jnp.int32) - 1) * route_marks, axis=1)
    targets = flat_ids * capacity + slot_ranks
    route_of_slot = jnp.full((slot_total,), route_total, jnp.int32).at[targets].set(route_index)
    occupied = route_of_slot < route_total
    clipped = jnp.minimum(route_of_slot, route_total - 1)
    source_rows = clipped // route_width
    slot_gates = jnp.where(
        occupied, gates.reshape(route_total)[clipped], jnp.zeros((), jnp.float32)
    )
    send_tokens = jnp.where(occupied[:, None], tokens[source_rows], jnp.zeros((), jnp.bfloat16))
    send_grads = (slot_gates[:, None] * grad_out[source_rows].astype(jnp.float32)).astype(
        jnp.bfloat16
    )
    recv_tokens, recv_grads = (
        lax.all_to_all(
            send_tokens.reshape(expert_count, capacity, model_width),
            "expert",
            split_axis=0,
            concat_axis=0,
            tiled=True,
        ),
        lax.all_to_all(
            send_grads.reshape(expert_count, capacity, model_width),
            "expert",
            split_axis=0,
            concat_axis=0,
            tiled=True,
        ),
    )
    slot_tokens = recv_tokens.reshape(slot_total, model_width)
    slot_grads = recv_grads.reshape(slot_total, model_width)
    local_in = w_in[0]
    local_down = w_down[0]
    full_in, full_down = (
        lax.all_gather(local_in, "dp", axis=0, tiled=True),
        lax.all_gather(local_down, "dp", axis=0, tiled=True),
    )
    preact = jnp.dot(slot_tokens, full_in, preferred_element_type=jnp.float32)
    grad_hidden = contract_last(slot_grads, full_down)
    pre_grad = pre_grads(preact, grad_hidden)
    slot_back = contract_last(pre_grad, full_in).astype(jnp.bfloat16)
    hidden_act = hidden_from(preact)
    columns = slot_tokens
    grad_in_local = lax.psum_scatter(
        contract_first(columns, pre_grad).astype(jnp.bfloat16),
        "dp",
        scatter_dimension=0,
        tiled=True,
    ).astype(jnp.float32)
    columns = hidden_act
    grad_down_local = lax.psum_scatter(
        contract_first(columns, slot_grads).astype(jnp.bfloat16),
        "dp",
        scatter_dimension=0,
        tiled=True,
    ).astype(jnp.float32)
    slot_return = lax.all_to_all(
        slot_back.reshape(expert_count, capacity, model_width),
        "expert",
        split_axis=0,
        concat_axis=0,
        tiled=True,
    )
    per_route = slot_return.reshape(slot_total, model_width)[targets]
    grad_tokens = jnp.sum(
        per_route.reshape(token_rows, route_width, model_width).astype(jnp.float32), axis=1
    ).astype(jnp.bfloat16)
    return (grad_tokens, grad_in_local[None], grad_down_local[None])


def fused_kernel(
    expert_count, capacity,
    ids_ref, gates_ref, tok_in, grad_in, win_in, wdn_in,
    z_in, gin_own, gin_recv, gdn_own, gdn_recv,
    data, meta, win, wdn, acc_dn, sel, xs, gs, act, dpre, part,
    sib_in, y_out, y_in, z_out, gin_send, gdn_send,
    local_sem, own_send, fwd_send, y_send, sib_send, recv_sem,
    w_send, w_recv, sib_part_send, sib_part_recv, y_part_send, y_part_recv,
    z_part_send, z_part_recv, g_send, g_recv,
):
    depth = expert_count // 4
    dp = lax.axis_index("dp")
    me = lax.axis_index("expert")
    z, y, c = me // 4, (me // 2) % 2, me % 2
    token_rows, model_width = tok_in.shape
    half_in, half_dn = win_in.shape[0], wdn_in.shape[0]
    half_width = wdn.shape[0]
    slots = 4 * capacity
    tile = model_width // 4

    def block_of(zz, yy, cc):
        return zz * 4 + yy * 2 + cc

    sib, y_peer = block_of(z, y, 1 - c), block_of(z, 1 - y, c)
    table = [sorted(range(depth), key=lambda b: (abs(b - zz), b)) for zz in range(depth)]

    def near(k):
        total = jnp.int32(0)
        for zz in range(depth):
            for kk in range(depth):
                hit = (z == zz).astype(jnp.int32) * (jnp.int32(k) == kk).astype(jnp.int32)
                total = total + hit * table[zz][kk]
        return total

    def data_copy(block, target, sems, piece):
        ref = meta.at[block] if piece == 2 else data.at[block, piece]
        return pltpu.make_async_remote_copy(
            src_ref=ref, dst_ref=ref,
            send_sem=sems.at[piece], recv_sem=recv_sem.at[block, piece],
            device_id=(dp, target), device_id_type=MESH)

    def ship(block, target, sems):
        for piece in range(3):
            data_copy(block, target, sems, piece).start()

    def sent(block, target, sems):
        for piece in range(3):
            data_copy(block, target, sems, piece).wait_send()

    def arrived(block):
        for piece in range(3):
            data_copy(block, sib, own_send.at[0], piece).wait_recv()

    own_rows_in = pl.ds(pl.multiple_of(dp * half_in, 16), half_in)
    own_rows_dn = pl.ds(pl.multiple_of(dp * half_dn, 16), half_dn)
    peer_rows_dn = pl.ds(pl.multiple_of((1 - dp) * half_dn, 16), half_dn)
    local = [
        pltpu.make_async_copy(tok_in, data.at[me, 0], local_sem.at[0]),
        pltpu.make_async_copy(grad_in, data.at[me, 1], local_sem.at[1]),
        pltpu.make_async_copy(win_in, win.at[own_rows_in], local_sem.at[2]),
        pltpu.make_async_copy(wdn_in, wdn.at[own_rows_dn], local_sem.at[3]),
    ]
    for copy in local:
        copy.start()

    barrier = pltpu.get_barrier_semaphore()
    partners = [(dp, sib), (dp, y_peer), (1 - dp, me)]
    for step in range(1, depth):
        partners.append((dp, block_of((z + step) % depth, y, c)))
    for partner in partners:
        pl.semaphore_signal(barrier, inc=1, device_id=partner, device_id_type=MESH)

    experts = lax.broadcasted_iota(jnp.int32, (expert_count, token_rows), 0)
    marks = jnp.zeros((expert_count, token_rows), F32)
    scale = jnp.zeros((expert_count, token_rows), F32)
    for k in range(ids_ref.shape[0]):
        hit = ids_ref[k : k + 1, :] == experts
        marks = marks + jnp.where(hit, 1.0, 0.0)
        scale = scale + jnp.where(hit, gates_ref[k : k + 1, :], 0.0)
    before = (
        lax.broadcasted_iota(jnp.int32, (token_rows, token_rows), 0)
        < lax.broadcasted_iota(jnp.int32, (token_rows, token_rows), 1)
    )
    ranks = jnp.dot(
        marks.astype(BF16), jnp.where(before, 1.0, 0.0).astype(BF16), preferred_element_type=F32
    )
    meta[me, 0:expert_count, :] = jnp.where(marks > 0.5, ranks, -1.0)
    meta[me, expert_count : 2 * expert_count, :] = scale

    pl.semaphore_wait(barrier, len(partners))

    weights = [
        pltpu.make_async_remote_copy(
            src_ref=src, dst_ref=dst, send_sem=w_send.at[i], recv_sem=w_recv.at[i],
            device_id=(1 - dp, me), device_id_type=MESH)
        for i, (src, dst) in enumerate(
            ((win_in, win.at[own_rows_in]), (wdn_in, wdn.at[own_rows_dn])))
    ]
    local[0].wait()
    local[1].wait()

    @pl.when(z > 0)
    def _():
        ship(me, block_of(jnp.maximum(z - 1, 0), y, c), own_send.at[0])

    @pl.when(z < depth - 1)
    def _():
        ship(me, block_of(jnp.minimum(z + 1, depth - 1), y, c), own_send.at[1])

    ship(me, y_peer, y_send.at[0])
    for copy in weights:
        copy.start()
    ship(me, sib, sib_send.at[0, 0])

    def onward(zz):
        step_to = jnp.where(zz < z, z + 1, z - 1)
        return (step_to >= 0) & (step_to < depth), jnp.clip(step_to, 0, depth - 1)

    def arrivals(k):
        zz = near(k)
        block = block_of(zz, y, c)
        more, step_to = onward(zz)
        for piece in range(3):
            data_copy(block, sib, own_send.at[0], piece).wait_recv()

            @pl.when(more)
            def _():
                data_copy(block, block_of(step_to, y, c), fwd_send.at[k], piece).start()

            data_copy(block, y_peer, y_send.at[k], piece).start()
            data_copy(block, sib, sib_send.at[k, 0], piece).start()

    def sib_part(k):
        return pltpu.make_async_remote_copy(
            src_ref=part.at[k, 1 - c], dst_ref=sib_in.at[k],
            send_sem=sib_part_send.at[k], recv_sem=sib_part_recv.at[k],
            device_id=(dp, sib), device_id_type=MESH)

    def y_part(k):
        return pltpu.make_async_remote_copy(
            src_ref=y_out.at[k], dst_ref=y_in.at[k],
            send_sem=y_part_send.at[k], recv_sem=y_part_recv.at[k],
            device_id=(dp, y_peer), device_id_type=MESH)

    def z_part(k, slot):
        return pltpu.make_async_remote_copy(
            src_ref=z_out.at[k], dst_ref=z_in.at[slot],
            send_sem=z_part_send.at[k], recv_sem=z_part_recv.at[slot],
            device_id=(dp, block_of(near(k), y, c)), device_id_type=MESH)

    def gin_part(i):
        rows = pl.ds(pl.multiple_of(i * tile, tile), tile)
        return pltpu.make_async_remote_copy(
            src_ref=gin_send.at[rows], dst_ref=gin_recv.at[rows],
            send_sem=g_send.at[i], recv_sem=g_recv.at[i],
            device_id=(1 - dp, me), device_id_type=MESH)

    half_tiles = half_in // tile
    keep = pltpu.make_async_copy(z_out.at[0], z_in.at[z], local_sem.at[4])

    def grad_in_rows(half, i):
        columns = pl.ds(pl.multiple_of(half * half_in + i * tile, tile), tile)
        return contract_first(xs[:, columns], dpre[...]).astype(BF16)

    gdn_part = pltpu.make_async_remote_copy(
        src_ref=gdn_send, dst_ref=gdn_recv,
        send_sem=g_send.at[half_tiles], recv_sem=g_recv.at[half_tiles],
        device_id=(1 - dp, me), device_id_type=MESH)

    def combine_y(k):
        sib_part(k).wait_recv()
        y_out[k] = (
            part[k, c, 1 - y].astype(F32) + sib_in[k, 1 - y].astype(F32)
        ).astype(BF16)
        y_part(k).start()

    def combine_z(k):
        y_part(k).wait_recv()
        z_out[k] = (
            part[k, c, y].astype(F32) + sib_in[k, y].astype(F32) + y_in[k].astype(F32)
        ).astype(BF16)

        if k > 0:
            z_part(k, z).start()
        else:
            keep.start()

    for k in range(1, min(3, depth)):
        arrivals(k)
    at_end = (z == 0) | (z == depth - 1)
    if depth > 3:
        @pl.when(~at_end)
        def _():
            arrivals(depth - 1)

    local[2].wait()
    local[3].wait()

    def chunk(k, carry):
        zz = near(k)
        if depth > 3:
            @pl.when((k == 1) & at_end)
            def _():
                arrivals(depth - 1)

        block = block_of(zz, 1 - y, c)
        arrived(block)
        ship(block, sib, sib_send.at[k, 1])
        arrived(block_of(zz, y, 1 - c))
        arrived(block_of(zz, 1 - y, 1 - c))

        @pl.when(k == 0)
        def _():
            for copy in weights:
                copy.wait_recv()

        last = k == depth - 1

        @pl.when(last)
        def _():
            for early in range(1, depth - 1):
                combine_y(early)

        first = zz * 4
        at_rows = pl.ds(pl.multiple_of(k * slots, 16), slots)
        slot_rows = lax.broadcasted_iota(jnp.int32, (slots, token_rows), 0)
        slot_gate = jnp.zeros((slots, 1), F32)
        for j in range(4):
            rank = meta[first + j, pl.ds(me, 1), :].astype(jnp.int32)
            place = jnp.where(rank >= 0, rank + j * capacity, -1)
            scale_row = meta[first + j, pl.ds(expert_count + me, 1), :]
            hit = slot_rows == place
            slot_gate = slot_gate + jnp.sum(
                jnp.where(hit, scale_row, 0.0), axis=1, keepdims=True
            )
            sel[:, j * token_rows : (j + 1) * token_rows] = jnp.where(hit, 1.0, 0.0).astype(BF16)
        chosen = sel[...]
        chunk_tokens = data[pl.ds(first, 4), 0].reshape(4 * token_rows, model_width)
        own_tokens = jnp.dot(chosen, chunk_tokens, preferred_element_type=F32).astype(BF16)
        xs[at_rows, :] = own_tokens
        chunk_grads = data[pl.ds(first, 4), 1].reshape(4 * token_rows, model_width)
        own_grads = (
            slot_gate * jnp.dot(chosen, chunk_grads, preferred_element_type=F32)
        ).astype(BF16)
        gs[at_rows, :] = own_grads
        preact = jnp.dot(xs[at_rows, :], win[...], preferred_element_type=F32)
        grad_hidden = contract_last(gs[at_rows, :], wdn[...])
        act[at_rows, :] = hidden_from(preact)
        dpre[at_rows, :] = pre_grads(preact, grad_hidden)

        @pl.when(last)
        def _():
            @pl.loop(0, half_tiles)
            def _(i):
                gin_send[pl.ds(pl.multiple_of(i * tile, tile), tile), :] = grad_in_rows(1 - dp, i)
                gin_part(i).start()

            acc_dn[...] = contract_first(act[...], gs[...])
            gdn_send[...] = acc_dn[peer_rows_dn, :].astype(BF16)
            gdn_part.start()

        back = contract_last(dpre[at_rows, :], win[...]).astype(BF16)
        spread = contract_first(sel[...], back).astype(BF16)
        for j in range(4):
            part[k, j % 2, j // 2] = spread[j * token_rows : (j + 1) * token_rows]
        sib_part(k).start()
        return carry

    lax.fori_loop(0, depth, chunk, 0)
    combine_y(depth - 1)
    for k in range(1, depth - 1):
        combine_z(k)
    combine_y(0)

    @pl.loop(0, half_tiles)
    def _(i):
        gin_own[pl.ds(pl.multiple_of(i * tile, tile), tile), :] = grad_in_rows(dp, i)

    combine_z(depth - 1)
    gdn_own[...] = acc_dn[own_rows_dn, :].astype(BF16)
    combine_z(0)
    for step in range(1, depth):
        z_part(step, (z + step) % depth).wait_recv()
    keep.wait()
    for i in range(half_tiles):
        gin_part(i).wait_recv()
    gdn_part.wait_recv()

    @pl.when(z > 0)
    def _():
        sent(me, sib, own_send.at[0])

    @pl.when(z < depth - 1)
    def _():
        sent(me, sib, own_send.at[1])

    for k in range(depth):
        sent(me, y_peer, y_send.at[k])
        sent(me, sib, sib_send.at[k, 0])
        sent(me, sib, sib_send.at[k, 1])
        sib_part(k).wait_send()
        y_part(k).wait_send()
        if k > 0:
            more, _ = onward(near(k))

            @pl.when(more)
            def _():
                sent(me, sib, fwd_send.at[k])

            z_part(k, z).wait_send()
    for copy in weights:
        copy.wait_send()
    for i in range(half_tiles):
        gin_part(i).wait_send()
    gdn_part.wait_send()


def fused_on_device(tokens, grad_out, expert_ids, gates, w_in, w_down):
    token_rows, model_width = tokens.shape
    route_total = token_rows * expert_ids.shape[1]
    expert_count = lax.axis_size("expert")
    capacity = route_total // expert_count + max(1, route_total // (8 * expert_count))
    depth = expert_count // 4
    slots = 4 * capacity
    half_in, in_width = w_in.shape[1:]
    half_dn = w_down.shape[1]
    half_tiles = half_in // (model_width // 4)
    dma = lambda *shape: pltpu.SemaphoreType.DMA(shape)
    vmem = lambda shape, dtype=BF16: pltpu.VMEM(shape, dtype)
    z_parts, own_in, other_in, own_dn, other_dn = pl.pallas_call(
        functools.partial(fused_kernel, expert_count, capacity),
        out_shape=(
            jax.ShapeDtypeStruct((depth, token_rows, model_width), BF16),
            jax.ShapeDtypeStruct((half_in, in_width), BF16),
            jax.ShapeDtypeStruct((half_in, in_width), BF16),
            jax.ShapeDtypeStruct((half_dn, model_width), BF16),
            jax.ShapeDtypeStruct((half_dn, model_width), BF16),
        ),
        in_specs=[pl.BlockSpec(memory_space=pltpu.VMEM)] * 2
        + [pl.BlockSpec(memory_space=pl.ANY)] * 4,
        out_specs=(
            pl.BlockSpec(memory_space=pl.ANY),
            pl.BlockSpec(memory_space=pltpu.VMEM),
            pl.BlockSpec(memory_space=pl.ANY),
            pl.BlockSpec(memory_space=pltpu.VMEM),
            pl.BlockSpec(memory_space=pl.ANY),
        ),
        scratch_shapes=[
            vmem((expert_count, 2, token_rows, model_width)),
            vmem((expert_count, 2 * expert_count, token_rows), F32),
            vmem((2 * half_in, in_width)),
            vmem((2 * half_dn, model_width)),
            vmem((2 * half_dn, model_width), F32),
            vmem((slots, 4 * token_rows)),
            vmem((depth * slots, model_width)),
            vmem((depth * slots, model_width)),
            vmem((depth * slots, in_width // 2)),
            vmem((depth * slots, in_width)),
            vmem((depth, 2, 2, token_rows, model_width)),
            vmem((depth, 2, token_rows, model_width)),
            vmem((depth, token_rows, model_width)),
            vmem((depth, token_rows, model_width)),
            vmem((depth, token_rows, model_width)),
            vmem((half_in, in_width)),
            vmem((half_dn, model_width)),
            dma(5), dma(2, 3), dma(depth, 3), dma(depth, 3), dma(depth, 2, 3),
            dma(expert_count, 3), dma(2), dma(2), dma(depth), dma(depth), dma(depth), dma(depth),
            dma(depth), dma(depth), dma(half_tiles + 1), dma(half_tiles + 1),
        ],
        compiler_params=pltpu.CompilerParams(
            collective_id=0, has_side_effects=True, vmem_limit_bytes=VMEM_BYTES
        ),
    )(expert_ids.T, gates.T, tokens, grad_out, w_in[0], w_down[0])
    grad_tokens = jnp.sum(z_parts.astype(F32), axis=0).astype(BF16)
    grad_in = own_in.astype(F32) + other_in.astype(F32)
    grad_down = own_dn.astype(F32) + other_dn.astype(F32)
    return grad_tokens, grad_in[None], grad_down[None]


def fits_fused(mesh):
    return mesh.shape["dp"] == 2 and mesh.shape["expert"] in (8, 16)


def solution(mesh):
    in_specs = (
        P(("dp", "expert"), None),
        P(("dp", "expert"), None),
        P(("dp", "expert"), None),
        P(("dp", "expert"), None),
        P("expert", "dp", None),
        P("expert", "dp", None),
    )
    out_specs = (P(("dp", "expert"), None), P("expert", "dp", None), P("expert", "dp", None))
    return jax.shard_map(
        fused_on_device if fits_fused(mesh) else on_device,
        mesh=mesh, in_specs=in_specs, out_specs=out_specs, check_vma=False
    )
```

```python
import functools

import jax
import jax.numpy as jnp
from jax import lax
from jax.experimental import pallas as pl
from jax.experimental.pallas import tpu as pltpu
from jax.sharding import PartitionSpec as P

MESH = pl.DeviceIdType.MESH
F32 = jnp.float32
BF16 = jnp.bfloat16
VMEM_BYTES = 56 * 1024 * 1024


def hidden_from(preact):
    half_width = preact.shape[1] // 2
    gate_pre = preact[:, :half_width]
    up_pre = preact[:, half_width:]
    sigmoid_gate = jax.nn.sigmoid(gate_pre)
    return (gate_pre * sigmoid_gate * up_pre).astype(jnp.bfloat16)


def pre_grads(preact, grad_hidden):
    half_width = preact.shape[1] // 2
    gate_pre = preact[:, :half_width]
    up_pre = preact[:, half_width:]
    sigmoid_gate = jax.nn.sigmoid(gate_pre)
    grad_gate = grad_hidden * up_pre * sigmoid_gate * (1.0 + gate_pre * (1.0 - sigmoid_gate))
    grad_up = grad_hidden * gate_pre * sigmoid_gate
    return jnp.concatenate([grad_gate, grad_up], axis=1).astype(jnp.bfloat16)


def contract_first(left, right):
    return lax.dot_general(
        left, right, (((0,), (0,)), ((), ())), preferred_element_type=jnp.float32
    )


def contract_last(left, right):
    return lax.dot_general(
        left, right, (((1,), (1,)), ((), ())), preferred_element_type=jnp.float32
    )


def on_device(tokens, grad_out, expert_ids, gates, w_in, w_down):
    token_rows, model_width = tokens.shape
    route_width = expert_ids.shape[1]
    expert_count = lax.axis_size("expert")
    route_total = token_rows * route_width
    capacity = route_total // expert_count + max(1, route_total // (8 * expert_count))
    slot_total = expert_count * capacity
    flat_ids = expert_ids.reshape(route_total)
    route_marks = (flat_ids[:, None] == jnp.arange(expert_count, dtype=jnp.int32)[None, :]).astype(
        jnp.int32
    )
    route_index = jnp.arange(route_total, dtype=jnp.int32)
    lower_table = (route_index[None, :] <= route_index[:, None]).astype(jnp.bfloat16)
    running = jnp.dot(
        lower_table, route_marks.astype(jnp.bfloat16), preferred_element_type=jnp.float32
    )
    slot_ranks = jnp.sum((running.astype(jnp.int32) - 1) * route_marks, axis=1)
    targets = flat_ids * capacity + slot_ranks
    route_of_slot = jnp.full((slot_total,), route_total, jnp.int32).at[targets].set(route_index)
    occupied = route_of_slot < route_total
    clipped = jnp.minimum(route_of_slot, route_total - 1)
    source_rows = clipped // route_width
    slot_gates = jnp.where(
        occupied, gates.reshape(route_total)[clipped], jnp.zeros((), jnp.float32)
    )
    send_tokens = jnp.where(occupied[:, None], tokens[source_rows], jnp.zeros((), jnp.bfloat16))
    send_grads = (slot_gates[:, None] * grad_out[source_rows].astype(jnp.float32)).astype(
        jnp.bfloat16
    )
    recv_tokens, recv_grads = (
        lax.all_to_all(
            send_tokens.reshape(expert_count, capacity, model_width),
            "expert",
            split_axis=0,
            concat_axis=0,
            tiled=True,
        ),
        lax.all_to_all(
            send_grads.reshape(expert_count, capacity, model_width),
            "expert",
            split_axis=0,
            concat_axis=0,
            tiled=True,
        ),
    )
    slot_tokens = recv_tokens.reshape(slot_total, model_width)
    slot_grads = recv_grads.reshape(slot_total, model_width)
    local_in = w_in[0]
    local_down = w_down[0]
    full_in, full_down = (
        lax.all_gather(local_in, "dp", axis=0, tiled=True),
        lax.all_gather(local_down, "dp", axis=0, tiled=True),
    )
    preact = jnp.dot(slot_tokens, full_in, preferred_element_type=jnp.float32)
    grad_hidden = contract_last(slot_grads, full_down)
    pre_grad = pre_grads(preact, grad_hidden)
    slot_back = contract_last(pre_grad, full_in).astype(jnp.bfloat16)
    hidden_act = hidden_from(preact)
    columns = slot_tokens
    grad_in_local = lax.psum_scatter(
        contract_first(columns, pre_grad).astype(jnp.bfloat16),
        "dp",
        scatter_dimension=0,
        tiled=True,
    ).astype(jnp.float32)
    columns = hidden_act
    grad_down_local = lax.psum_scatter(
        contract_first(columns, slot_grads).astype(jnp.bfloat16),
        "dp",
        scatter_dimension=0,
        tiled=True,
    ).astype(jnp.float32)
    slot_return = lax.all_to_all(
        slot_back.reshape(expert_count, capacity, model_width),
        "expert",
        split_axis=0,
        concat_axis=0,
        tiled=True,
    )
    per_route = slot_return.reshape(slot_total, model_width)[targets]
    grad_tokens = jnp.sum(
        per_route.reshape(token_rows, route_width, model_width).astype(jnp.float32), axis=1
    ).astype(jnp.bfloat16)
    return (grad_tokens, grad_in_local[None], grad_down_local[None])


def fused_kernel(
    expert_count, capacity,
    ids_ref, gates_ref, tok_in, grad_in, win_in, wdn_in,
    z_in, gin_own, gin_recv, gdn_own, gdn_recv,
    data, meta, win, wdn, acc_dn, sel, xs, gs, act, dpre, part,
    sib_in, y_out, y_in, z_out, gin_send, gdn_send,
    local_sem, own_send, fwd_send, y_send, sib_send, recv_sem,
    w_send, w_recv, sib_part_send, sib_part_recv, y_part_send, y_part_recv,
    z_part_send, z_part_recv, g_send, g_recv,
):
    depth = expert_count // 4
    dp = lax.axis_index("dp")
    me = lax.axis_index("expert")
    z, y, c = me // 4, (me // 2) % 2, me % 2
    token_rows, model_width = tok_in.shape
    half_in, half_dn = win_in.shape[0], wdn_in.shape[0]
    half_width = wdn.shape[0]
    slots = 4 * capacity
    tile = model_width // 4

    def block_of(zz, yy, cc):
        return zz * 4 + yy * 2 + cc

    sib, y_peer = block_of(z, y, 1 - c), block_of(z, 1 - y, c)
    table = [sorted(range(depth), key=lambda b: (abs(b - zz), b)) for zz in range(depth)]

    def near(k):
        total = jnp.int32(0)
        for zz in range(depth):
            for kk in range(depth):
                hit = (z == zz).astype(jnp.int32) * (jnp.int32(k) == kk).astype(jnp.int32)
                total = total + hit * table[zz][kk]
        return total

    def data_copy(block, target, sems, piece):
        ref = meta.at[block] if piece == 2 else data.at[block, piece]
        return pltpu.make_async_remote_copy(
            src_ref=ref, dst_ref=ref,
            send_sem=sems.at[piece], recv_sem=recv_sem.at[block, piece],
            device_id=(dp, target), device_id_type=MESH)

    def ship(block, target, sems):
        for piece in range(3):
            data_copy(block, target, sems, piece).start()

    def sent(block, target, sems):
        for piece in range(3):
            data_copy(block, target, sems, piece).wait_send()

    def arrived(block):
        for piece in range(3):
            data_copy(block, sib, own_send.at[0], piece).wait_recv()

    own_rows_in = pl.ds(pl.multiple_of(dp * half_in, 16), half_in)
    own_rows_dn = pl.ds(pl.multiple_of(dp * half_dn, 16), half_dn)
    peer_rows_dn = pl.ds(pl.multiple_of((1 - dp) * half_dn, 16), half_dn)
    local = [
        pltpu.make_async_copy(tok_in, data.at[me, 0], local_sem.at[0]),
        pltpu.make_async_copy(grad_in, data.at[me, 1], local_sem.at[1]),
        pltpu.make_async_copy(win_in, win.at[own_rows_in], local_sem.at[2]),
        pltpu.make_async_copy(wdn_in, wdn.at[own_rows_dn], local_sem.at[3]),
    ]
    for copy in local:
        copy.start()

    barrier = pltpu.get_barrier_semaphore()
    partners = [(dp, sib), (dp, y_peer), (1 - dp, me)]
    for step in range(1, depth):
        partners.append((dp, block_of((z + step) % depth, y, c)))
    for partner in partners:
        pl.semaphore_signal(barrier, inc=1, device_id=partner, device_id_type=MESH)

    experts = lax.broadcasted_iota(jnp.int32, (expert_count, token_rows), 0)
    marks = jnp.zeros((expert_count, token_rows), F32)
    scale = jnp.zeros((expert_count, token_rows), F32)
    for k in range(ids_ref.shape[0]):
        hit = ids_ref[k : k + 1, :] == experts
        marks = marks + jnp.where(hit, 1.0, 0.0)
        scale = scale + jnp.where(hit, gates_ref[k : k + 1, :], 0.0)
    before = (
        lax.broadcasted_iota(jnp.int32, (token_rows, token_rows), 0)
        < lax.broadcasted_iota(jnp.int32, (token_rows, token_rows), 1)
    )
    ranks = jnp.dot(
        marks.astype(BF16), jnp.where(before, 1.0, 0.0).astype(BF16), preferred_element_type=F32
    )
    meta[me, 0:expert_count, :] = jnp.where(marks > 0.5, ranks, -1.0)
    meta[me, expert_count : 2 * expert_count, :] = scale

    pl.semaphore_wait(barrier, len(partners))

    weights = [
        pltpu.make_async_remote_copy(
            src_ref=src, dst_ref=dst, send_sem=w_send.at[i], recv_sem=w_recv.at[i],
            device_id=(1 - dp, me), device_id_type=MESH)
        for i, (src, dst) in enumerate(
            ((win_in, win.at[own_rows_in]), (wdn_in, wdn.at[own_rows_dn])))
    ]
    local[0].wait()
    local[1].wait()

    @pl.when(z > 0)
    def _():
        ship(me, block_of(jnp.maximum(z - 1, 0), y, c), own_send.at[0])

    @pl.when(z < depth - 1)
    def _():
        ship(me, block_of(jnp.minimum(z + 1, depth - 1), y, c), own_send.at[1])

    ship(me, y_peer, y_send.at[0])
    for copy in weights:
        copy.start()
    ship(me, sib, sib_send.at[0, 0])

    def onward(zz):
        step_to = jnp.where(zz < z, z + 1, z - 1)
        return (step_to >= 0) & (step_to < depth), jnp.clip(step_to, 0, depth - 1)

    def arrivals(k):
        zz = near(k)
        block = block_of(zz, y, c)
        more, step_to = onward(zz)
        for piece in range(3):
            data_copy(block, sib, own_send.at[0], piece).wait_recv()

            @pl.when(more)
            def _():
                data_copy(block, block_of(step_to, y, c), fwd_send.at[k], piece).start()

            data_copy(block, y_peer, y_send.at[k], piece).start()
            data_copy(block, sib, sib_send.at[k, 0], piece).start()

    def sib_part(k):
        return pltpu.make_async_remote_copy(
            src_ref=part.at[k, 1 - c], dst_ref=sib_in.at[k],
            send_sem=sib_part_send.at[k], recv_sem=sib_part_recv.at[k],
            device_id=(dp, sib), device_id_type=MESH)

    def y_part(k):
        return pltpu.make_async_remote_copy(
            src_ref=y_out.at[k], dst_ref=y_in.at[k],
            send_sem=y_part_send.at[k], recv_sem=y_part_recv.at[k],
            device_id=(dp, y_peer), device_id_type=MESH)

    def z_part(k, slot):
        return pltpu.make_async_remote_copy(
            src_ref=z_out.at[k], dst_ref=z_in.at[slot],
            send_sem=z_part_send.at[k], recv_sem=z_part_recv.at[slot],
            device_id=(dp, block_of(near(k), y, c)), device_id_type=MESH)

    def gin_part(i):
        rows = pl.ds(pl.multiple_of(i * tile, tile), tile)
        return pltpu.make_async_remote_copy(
            src_ref=gin_send.at[rows], dst_ref=gin_recv.at[rows],
            send_sem=g_send.at[i], recv_sem=g_recv.at[i],
            device_id=(1 - dp, me), device_id_type=MESH)

    half_tiles = half_in // tile
    keep = pltpu.make_async_copy(z_out.at[0], z_in.at[z], local_sem.at[4])

    def grad_in_rows(half, i):
        columns = pl.ds(pl.multiple_of(half * half_in + i * tile, tile), tile)
        return contract_first(xs[:, columns], dpre[...]).astype(BF16)

    gdn_part = pltpu.make_async_remote_copy(
        src_ref=gdn_send, dst_ref=gdn_recv,
        send_sem=g_send.at[half_tiles], recv_sem=g_recv.at[half_tiles],
        device_id=(1 - dp, me), device_id_type=MESH)

    def sum_y(k):
        sib_part(k).wait_recv()
        y_out[k] = (
            part[k, c, 1 - y].astype(F32) + sib_in[k, 1 - y].astype(F32)
        ).astype(BF16)

    def combine_y(k):
        sum_y(k)
        y_part(k).start()

    def combine_z(k):
        y_part(k).wait_recv()
        z_out[k] = (
            part[k, c, y].astype(F32) + sib_in[k, y].astype(F32) + y_in[k].astype(F32)
        ).astype(BF16)

        if k > 0:
            z_part(k, z).start()
        else:
            keep.start()

    for k in range(1, min(3, depth)):
        arrivals(k)
    at_end = (z == 0) | (z == depth - 1)
    if depth > 3:
        @pl.when(~at_end)
        def _():
            arrivals(depth - 1)

    local[2].wait()
    local[3].wait()

    def chunk(k, carry):
        zz = near(k)
        if depth > 3:
            @pl.when((k == 1) & at_end)
            def _():
                arrivals(depth - 1)

        last = k == depth - 1

        @pl.when(last)
        def _():
            for early in range(1, depth - 1):
                sum_y(early)

        block = block_of(zz, 1 - y, c)
        for piece in range(3):
            data_copy(block, sib, own_send.at[0], piece).wait_recv()
            data_copy(block, sib, sib_send.at[k, 1], piece).start()
        arrived(block_of(zz, y, 1 - c))
        arrived(block_of(zz, 1 - y, 1 - c))

        @pl.when(k == 0)
        def _():
            for copy in weights:
                copy.wait_recv()

        @pl.when(last)
        def _():
            for early in range(1, depth - 1):
                y_part(early).start()

        first = zz * 4
        at_rows = pl.ds(pl.multiple_of(k * slots, 16), slots)
        slot_rows = lax.broadcasted_iota(jnp.int32, (slots, token_rows), 0)
        slot_gate = jnp.zeros((slots, 1), F32)
        for j in range(4):
            rank = meta[first + j, pl.ds(me, 1), :].astype(jnp.int32)
            place = jnp.where(rank >= 0, rank + j * capacity, -1)
            scale_row = meta[first + j, pl.ds(expert_count + me, 1), :]
            hit = slot_rows == place
            slot_gate = slot_gate + jnp.sum(
                jnp.where(hit, scale_row, 0.0), axis=1, keepdims=True
            )
            sel[:, j * token_rows : (j + 1) * token_rows] = jnp.where(hit, 1.0, 0.0).astype(BF16)
        chosen = sel[...]
        chunk_tokens = data[pl.ds(first, 4), 0].reshape(4 * token_rows, model_width)
        own_tokens = jnp.dot(chosen, chunk_tokens, preferred_element_type=F32).astype(BF16)
        xs[at_rows, :] = own_tokens
        chunk_grads = data[pl.ds(first, 4), 1].reshape(4 * token_rows, model_width)
        own_grads = (
            slot_gate * jnp.dot(chosen, chunk_grads, preferred_element_type=F32)
        ).astype(BF16)
        gs[at_rows, :] = own_grads
        preact = jnp.dot(xs[at_rows, :], win[...], preferred_element_type=F32)
        grad_hidden = contract_last(gs[at_rows, :], wdn[...])
        act[at_rows, :] = hidden_from(preact)
        dpre[at_rows, :] = pre_grads(preact, grad_hidden)

        @pl.when(last)
        def _():
            @pl.loop(0, half_tiles)
            def _(i):
                gin_send[pl.ds(pl.multiple_of(i * tile, tile), tile), :] = grad_in_rows(1 - dp, i)
                gin_part(i).start()

            acc_dn[...] = contract_first(act[...], gs[...])
            gdn_send[...] = acc_dn[peer_rows_dn, :].astype(BF16)
            gdn_part.start()

        back = contract_last(dpre[at_rows, :], win[...]).astype(BF16)
        spread = contract_first(sel[...], back).astype(BF16)
        for j in range(4):
            part[k, j % 2, j // 2] = spread[j * token_rows : (j + 1) * token_rows]
        sib_part(k).start()
        return carry

    lax.fori_loop(0, depth, chunk, 0)
    combine_y(depth - 1)
    for k in range(1, depth - 1):
        combine_z(k)
    combine_y(0)

    @pl.loop(0, half_tiles)
    def _(i):
        gin_own[pl.ds(pl.multiple_of(i * tile, tile), tile), :] = grad_in_rows(dp, i)

    combine_z(depth - 1)
    gdn_own[...] = acc_dn[own_rows_dn, :].astype(BF16)
    combine_z(0)
    for step in range(1, depth):
        z_part(step, (z + step) % depth).wait_recv()
    keep.wait()
    for i in range(half_tiles):
        gin_part(i).wait_recv()
    gdn_part.wait_recv()

    @pl.when(z > 0)
    def _():
        sent(me, sib, own_send.at[0])

    @pl.when(z < depth - 1)
    def _():
        sent(me, sib, own_send.at[1])

    for k in range(depth):
        sent(me, y_peer, y_send.at[k])
        sent(me, sib, sib_send.at[k, 0])
        sent(me, sib, sib_send.at[k, 1])
        sib_part(k).wait_send()
        y_part(k).wait_send()
        if k > 0:
            more, _ = onward(near(k))

            @pl.when(more)
            def _():
                sent(me, sib, fwd_send.at[k])

            z_part(k, z).wait_send()
    for copy in weights:
        copy.wait_send()
    for i in range(half_tiles):
        gin_part(i).wait_send()
    gdn_part.wait_send()


def fused_on_device(tokens, grad_out, expert_ids, gates, w_in, w_down):
    token_rows, model_width = tokens.shape
    route_total = token_rows * expert_ids.shape[1]
    expert_count = lax.axis_size("expert")
    capacity = route_total // expert_count + max(1, route_total // (8 * expert_count))
    depth = expert_count // 4
    slots = 4 * capacity
    half_in, in_width = w_in.shape[1:]
    half_dn = w_down.shape[1]
    half_tiles = half_in // (model_width // 4)
    dma = lambda *shape: pltpu.SemaphoreType.DMA(shape)
    vmem = lambda shape, dtype=BF16: pltpu.VMEM(shape, dtype)
    z_parts, own_in, other_in, own_dn, other_dn = pl.pallas_call(
        functools.partial(fused_kernel, expert_count, capacity),
        out_shape=(
            jax.ShapeDtypeStruct((depth, token_rows, model_width), BF16),
            jax.ShapeDtypeStruct((half_in, in_width), BF16),
            jax.ShapeDtypeStruct((half_in, in_width), BF16),
            jax.ShapeDtypeStruct((half_dn, model_width), BF16),
            jax.ShapeDtypeStruct((half_dn, model_width), BF16),
        ),
        in_specs=[pl.BlockSpec(memory_space=pltpu.VMEM)] * 2
        + [pl.BlockSpec(memory_space=pl.ANY)] * 4,
        out_specs=(
            pl.BlockSpec(memory_space=pl.ANY),
            pl.BlockSpec(memory_space=pltpu.VMEM),
            pl.BlockSpec(memory_space=pl.ANY),
            pl.BlockSpec(memory_space=pltpu.VMEM),
            pl.BlockSpec(memory_space=pl.ANY),
        ),
        scratch_shapes=[
            vmem((expert_count, 2, token_rows, model_width)),
            vmem((expert_count, 2 * expert_count, token_rows), F32),
            vmem((2 * half_in, in_width)),
            vmem((2 * half_dn, model_width)),
            vmem((2 * half_dn, model_width), F32),
            vmem((slots, 4 * token_rows)),
            vmem((depth * slots, model_width)),
            vmem((depth * slots, model_width)),
            vmem((depth * slots, in_width // 2)),
            vmem((depth * slots, in_width)),
            vmem((depth, 2, 2, token_rows, model_width)),
            vmem((depth, 2, token_rows, model_width)),
            vmem((depth, token_rows, model_width)),
            vmem((depth, token_rows, model_width)),
            vmem((depth, token_rows, model_width)),
            vmem((half_in, in_width)),
            vmem((half_dn, model_width)),
            dma(5), dma(2, 3), dma(depth, 3), dma(depth, 3), dma(depth, 2, 3),
            dma(expert_count, 3), dma(2), dma(2), dma(depth), dma(depth), dma(depth), dma(depth),
            dma(depth), dma(depth), dma(half_tiles + 1), dma(half_tiles + 1),
        ],
        compiler_params=pltpu.CompilerParams(
            collective_id=0, has_side_effects=True, vmem_limit_bytes=VMEM_BYTES
        ),
    )(expert_ids.T, gates.T, tokens, grad_out, w_in[0], w_down[0])
    grad_tokens = jnp.sum(z_parts.astype(F32), axis=0).astype(BF16)
    grad_in = own_in.astype(F32) + other_in.astype(F32)
    grad_down = own_dn.astype(F32) + other_dn.astype(F32)
    return grad_tokens, grad_in[None], grad_down[None]


def fits_fused(mesh):
    return mesh.shape["dp"] == 2 and mesh.shape["expert"] in (8, 16)


def solution(mesh):
    in_specs = (
        P(("dp", "expert"), None),
        P(("dp", "expert"), None),
        P(("dp", "expert"), None),
        P(("dp", "expert"), None),
        P("expert", "dp", None),
        P("expert", "dp", None),
    )
    out_specs = (P(("dp", "expert"), None), P("expert", "dp", None), P("expert", "dp", None))
    return jax.shard_map(
        fused_on_device if fits_fused(mesh) else on_device,
        mesh=mesh, in_specs=in_specs, out_specs=out_specs, check_vma=False
    )
```
